128 devices in a mesh: ctx: 64 (over x, z, y), wa: 2 (over core).
Axes of the slice: x: 4, y: 4, z: 4, core: 2. Of those that a mesh axis runs over, the one named last changes fastest.
Arguments:
- tokens: bfloat16 [8192, 1600], P('ctx'), may hold values from -6 to 6
- norm_gain: float32 [1600], replicated, may hold values from 0.25 to 1.75
- qkv_weight: bfloat16 [1600, 2240], P('ctx'), may hold values from -0.15625 to 0.15625
- heads_gain: float32 [1600], replicated, may hold values from 0.25 to 1.75
- mamba_in: bfloat16 [1600, 2, 3200], P('ctx', None, 'wa'), may hold values from -0.15625 to 0.15625
- conv_weight: bfloat16 [4, 3200], P(None, 'wa'), may hold values from -3 to 3
- conv_bias: float32 [3200], P('wa'), may hold values from -4 to 4
- state_proj: bfloat16 [3200, 132], P('wa'), may hold values from -0.109375 to 0.109375
- step_proj: bfloat16 [100, 3200], P(None, 'wa'), may hold values from -0.625 to 0.625
- step_bias: float32 [3200], P('wa'), may hold values from -4 to 0
- decay_log: float32 [3200, 16], P('wa'), may hold values from -9 to 0
- skip_gain: float32 [3200], P('wa'), may hold values from 0.5 to 3
- mamba_gain: float32 [3200], P('wa'), may hold values from 0.25 to 1.75
- heads_out: bfloat16 [1600, 1600], P('ctx', 'wa'), may hold values from -0.15625 to 0.15625
- mamba_out: bfloat16 [1600, 3200], P('ctx', 'wa'), may hold values from -0.109375 to 0.109375
- mlp_gain: float32 [1600], replicated, may hold values from 0.25 to 1.75
- gate_up: bfloat16 [1600, 2, 5504], P('ctx', None, 'wa'), may hold values from -0.15625 to 0.15625
- down_proj: bfloat16 [1600, 5504], P('ctx', 'wa'), may hold values from -0.078125 to 0.078125
- cotangent: bfloat16 [8192, 1600], P('ctx'), may hold values from -16 to 16
Outputs:
- layer_out: bfloat16 [8192, 1600], P('ctx')
- tokens_grad: float32 [8192, 1600], P('ctx')
- norm_gain_grad: float32 [1600], replicated
- qkv_weight_grad: float32 [1600, 2240], P('ctx')
- heads_gain_grad: float32 [1600], replicated
- mamba_in_grad: float32 [1600, 2, 3200], P('ctx', None, 'wa')
- conv_weight_grad: float32 [4, 3200], P(None, 'wa')
- conv_bias_grad: float32 [3200], P('wa')
- state_proj_grad: float32 [3200, 132], P('wa')
- step_proj_grad: float32 [100, 3200], P(None, 'wa')
- step_bias_grad: float32 [3200], P('wa')
- decay_log_grad: float32 [3200, 16], P('wa')
- skip_gain_grad: float32 [3200], P('wa')
- mamba_gain_grad: float32 [3200], P('wa')
- heads_out_grad: float32 [1600, 1600], P('ctx', 'wa')
- mamba_out_grad: float32 [1600, 3200], P('ctx', 'wa')
- mlp_gain_grad: float32 [1600], replicated
- gate_up_grad: float32 [1600, 2, 5504], P('ctx', None, 'wa')
- down_proj_grad: float32 [1600, 5504], P('ctx', 'wa')
The draws below stay inside these ranges and needn't reach their ends.
All inputs are finite; a program needn't handle non-finite values.
Results may differ from the reference program's by a relative error of at most 0.014.
Values may be sent and summed in bfloat16 or wider, within the bound.
No kernel may reach another device: no remote copies, remote signals or barrier semaphores. Data moves between devices by JAX's collectives and lax.ppermute only.
A program may use at most 576 MiB of HBM per device.

```python
import math
import jax
import jax.numpy as jnp
from jax import lax

D = 1600
KV_HEADS = 5
GROUP = 5
HEAD = 64
INNER = 3200
STATE = 16
RANK = 100
FF = 5504
CONV = 4
WINDOW = 1024
TOKENS = 8192
ATT = 1600
KVW = 320


def spiked(drawn, stream_key, source, target, shards_of, factor):
    def block_of(dim):
        return (jnp.arange(drawn.shape[dim]) // (drawn.shape[dim] // shards_of)).reshape((-1,) + (1,) * (drawn.ndim - 1 - dim))

    one_side = jax.random.permutation(stream_key, shards_of)[block_of(target)]
    far = (block_of(target) + shards_of // 2) % shards_of
    return jnp.where((block_of(source) == one_side) | (block_of(source) == far), factor * drawn, drawn)


def shard_levels(rng, shape, split, low, top_value):
    def one(dim, shards_of):
        steps = jax.random.uniform(jax.random.fold_in(jax.random.fold_in(rng, 6), dim), (shards_of,), jnp.float32, low / len(split), top_value / len(split))
        return jnp.repeat(jnp.exp(steps), shape[dim] // shards_of).reshape((-1,) + (1,) * (len(shape) - dim - 1))

    factor_of = one(*split[0])
    for cut in split[1:]:
        factor_of = factor_of * one(*cut)
    return factor_of


def centred(stream_key, extent, width, most, pieces=(), kind=jnp.bfloat16):
    loudness = shard_levels(stream_key, extent, pieces, -0.22, 0.18) if pieces else 1.0
    drawn = jax.random.normal(stream_key, extent, jnp.float32) * width * loudness
    return jnp.minimum(jnp.maximum(drawn, -most), most).astype(kind)


def heavy_noise(own_key, shape, deviation, most, cuts, heavy, kind=jnp.bfloat16):
    values = deviation * jax.random.normal(own_key, shape, jnp.float32)
    if cuts:
        values = values * shard_levels(own_key, shape, cuts, -0.22, 0.18)
    return jnp.clip(spiked(values, jax.random.fold_in(own_key, 3), *heavy), -most, most).astype(kind)


def setup_inputs(seed: int = 0) -> dict:
    keys = jax.random.split(jax.random.key(seed), 20)
    tokens = centred(keys[0], (TOKENS, D), 1.0, 6.0, ((0, 64),))
    norm_gain = jnp.clip(1.0 + 0.15 * jax.random.normal(keys[1], (D,), jnp.float32), 0.25, 1.75)
    qkv_weight = centred(keys[2], (D, ATT + 2 * KVW), D ** -0.5, 0.15625, ((0, 64),))
    heads_gain = jnp.clip(1.0 + 0.15 * jax.random.normal(keys[3], (ATT,), jnp.float32), 0.25, 1.75)
    mamba_in = centred(keys[4], (D, 2, INNER), D ** -0.5, 0.15625, ((0, 64), (2, 2)))
    conv_weight = centred(keys[5], (CONV, INNER), CONV ** -0.5, 3.0, ((1, 2),))
    conv_bias = centred(keys[6], (INNER,), 0.3, 4.0, ((0, 2),), jnp.float32)
    state_proj = centred(keys[7], (INNER, RANK + 2 * STATE), INNER ** -0.5, 0.109375, ((0, 2),))
    step_proj = centred(keys[8], (RANK, INNER), RANK ** -0.5, 0.625, ((1, 2),))
    step_bias = jnp.clip(-4.0 + 4.0 * jax.random.uniform(keys[9], (INNER,), jnp.float32) ** shard_levels(keys[9], (INNER,), ((0, 2),), -0.2, 0.2), -4.0, 0.0)
    decay_log = jnp.clip(-9.0 + 9.0 * jax.random.uniform(keys[10], (INNER, STATE), jnp.float32) ** shard_levels(keys[10], (INNER, STATE), ((0, 2),), -0.2, 0.2), -9.0, 0.0)
    skip_gain = jnp.clip(0.5 + 2.5 * jax.random.uniform(keys[11], (INNER,), jnp.float32) ** shard_levels(keys[11], (INNER,), ((0, 2),), -0.2, 0.2), 0.5, 3.0)
    mamba_gain = jnp.clip(1.0 + 0.15 * jax.random.normal(keys[12], (INNER,), jnp.float32), 0.25, 1.75)
    heads_out = centred(keys[13], (D, ATT), ATT ** -0.5, 0.15625, ((0, 64), (1, 2)))
    mamba_out = centred(keys[14], (D, INNER), INNER ** -0.5, 0.109375, ((0, 64), (1, 2)))
    mlp_gain = jnp.clip(1.0 + 0.15 * jax.random.normal(keys[15], (D,), jnp.float32), 0.25, 1.75)
    gate_up = centred(keys[16], (D, 2, FF), D ** -0.5, 0.15625, ((0, 64), (2, 2)))
    down_proj = centred(keys[17], (D, FF), FF ** -0.5, 0.078125, ((0, 64), (1, 2)))
    cotangent = heavy_noise(keys[18], (TOKENS, D), 1.0, 16.0, ((0, 64),), (0, 1, 64, 4.0))
    return {"tokens": tokens, "norm_gain": norm_gain, "qkv_weight": qkv_weight, "heads_gain": heads_gain, "mamba_in": mamba_in, "conv_weight": conv_weight, "conv_bias": conv_bias, "state_proj": state_proj, "step_proj": step_proj, "step_bias": step_bias, "decay_log": decay_log, "skip_gain": skip_gain, "mamba_gain": mamba_gain, "heads_out": heads_out, "mamba_out": mamba_out, "mlp_gain": mlp_gain, "gate_up": gate_up, "down_proj": down_proj, "cotangent": cotangent}


@jax.custom_vjp
def low(v):
    return lax.optimization_barrier(v.astype(jnp.bfloat16)).astype(jnp.float32)

@jax.custom_vjp
def low_back(v):
    return v

def low_keep(v):
    return (low(v), None)

def low_pass(kept, grad):
    return (grad,)

def back_keep(v):
    return (v, None)

def back_low(kept, grad):
    return (low(grad),)
low.defvjp(low_keep, low_pass)
low_back.defvjp(back_keep, back_low)
epsilon = 1e-06
highest = lax.Precision.HIGHEST

def matmul(left, right):
    return jnp.dot(left, right, precision=highest, preferred_element_type=jnp.float32)

def norm_apply(values, gain):
    return values * lax.rsqrt(lax.optimization_barrier(jnp.mean(values * values, -1, keepdims=True)) + epsilon) * gain

def attend(queries, keys_all, values_all):
    total_rows = queries.shape[0]
    query_block = math.gcd(total_rows, 512)
    kv_width = keys_all.shape[1]
    zero_rows = jnp.zeros((WINDOW, kv_width), jnp.float32)
    keys_pad = jnp.concatenate((zero_rows, keys_all), 0)
    values_pad = jnp.concatenate((zero_rows, values_all), 0)
    score_scale = HEAD ** (-0.5)

    def one_block(first_pos):
        block_queries = lax.dynamic_slice_in_dim(queries, first_pos, query_block, 0).reshape(query_block, KV_HEADS, GROUP, HEAD)
        block_keys = lax.dynamic_slice_in_dim(keys_pad, first_pos, query_block + WINDOW, 0).reshape(query_block + WINDOW, KV_HEADS, HEAD)
        block_values = lax.dynamic_slice_in_dim(values_pad, first_pos, query_block + WINDOW, 0).reshape(query_block + WINDOW, KV_HEADS, HEAD)
        scores = low_back(jnp.einsum('tkgd,skd->kgts', block_queries, block_keys, precision=highest) * score_scale)
        query_pos = first_pos + jnp.arange(query_block, dtype=jnp.int32)
        key_pos = first_pos - WINDOW + jnp.arange(query_block + WINDOW, dtype=jnp.int32)
        visible = (key_pos[None, :] <= query_pos[:, None]) & (key_pos[None, :] > query_pos[:, None] - WINDOW) & (key_pos[None, :] >= 0)
        masked = jnp.where(visible, scores, -1e+30)
        row_max = lax.optimization_barrier(jnp.max(masked, -1, keepdims=True))
        lifted = jnp.exp(masked - row_max)
        probability = low(lifted / lax.optimization_barrier(jnp.sum(lifted, -1, keepdims=True)))
        mixed_heads = jnp.einsum('kgts,skd->tkgd', probability, block_values, precision=highest)
        return mixed_heads.reshape(query_block, KV_HEADS * GROUP * HEAD)
    starts = jnp.arange(total_rows // query_block, dtype=jnp.int32) * query_block
    return lax.map(jax.checkpoint(one_block), starts).reshape(total_rows, KV_HEADS * GROUP * HEAD)

def conv_act(conv_in, conv_weight, conv_bias):
    total_rows = conv_in.shape[0]
    pad_rows = jnp.zeros((CONV - 1, conv_in.shape[1]), jnp.float32)
    extended = jnp.concatenate((pad_rows, conv_in), 0)
    summed = conv_bias + conv_weight[0] * extended[0:total_rows]
    for offset in range(1, CONV):
        summed = summed + conv_weight[offset] * extended[offset:offset + total_rows]
    return jax.nn.silu(summed)

def state_scan(acted, step_sizes, input_mat, output_mat, decay_log):
    total_rows = acted.shape[0]
    block_rows = math.gcd(total_rows, 256)
    block_count = total_rows // block_rows
    decay_rates = -jnp.exp(decay_log)

    def one_step(carry_state, entries):
        acted_now, step_now, input_now, output_now = entries
        carry_state = jnp.exp(step_now[:, None] * decay_rates) * carry_state + (step_now * acted_now)[:, None] * input_now[None, :]
        return (carry_state, lax.optimization_barrier(jnp.sum(carry_state * output_now[None, :], -1)))

    def one_block(carry_state, entries):
        return lax.scan(one_step, carry_state, entries)
    entries = (acted.reshape(block_count, block_rows, INNER), step_sizes.reshape(block_count, block_rows, INNER), input_mat.reshape(block_count, block_rows, STATE), output_mat.reshape(block_count, block_rows, STATE))
    start_state = jnp.zeros((INNER, STATE), jnp.float32)
    final_state, outputs = lax.scan(jax.checkpoint(one_block), start_state, entries)
    return outputs.reshape(total_rows, INNER)

def forward(tokens, norm_gain, qkv_weight, heads_gain, mamba_in, conv_weight, conv_bias, state_proj, step_proj, step_bias, decay_log, skip_gain, mamba_gain, heads_out, mamba_out, mlp_gain, gate_up, down_proj):
    heads_width = KV_HEADS * GROUP * HEAD
    kv_width = KV_HEADS * HEAD
    normed = low(norm_apply(tokens, norm_gain))
    projected = low(low_back(matmul(normed, qkv_weight)))
    heads_value = low_back(attend(projected[:, :heads_width], projected[:, heads_width:heads_width + kv_width], projected[:, heads_width + kv_width:]))
    heads_normed = low(norm_apply(heads_value, heads_gain))
    mixed_in = low(low_back(matmul(normed, mamba_in.reshape(D, 2 * INNER))))
    conv_in = mixed_in[:, :INNER]
    gate_in = mixed_in[:, INNER:]
    acted = low(conv_act(conv_in, conv_weight, conv_bias))
    state_in = low_back(matmul(acted, state_proj))
    low_rank = low(state_in[:, :RANK])
    input_mat = state_in[:, RANK:RANK + STATE]
    output_mat = state_in[:, RANK + STATE:]
    step_sizes = jax.nn.softplus(low_back(matmul(low_rank, step_proj)) + step_bias)
    ssm_value = state_scan(acted, step_sizes, input_mat, output_mat, decay_log) + skip_gain * acted
    gated = ssm_value * jax.nn.silu(gate_in)
    mamba_normed = low(norm_apply(gated, mamba_gain))
    mixer = low_back((matmul(heads_normed, heads_out.T) + matmul(mamba_normed, mamba_out.T)) * 0.5)
    middle = tokens + mixer
    normed_mid = low(norm_apply(middle, mlp_gain))
    gate_values = low_back(matmul(normed_mid, gate_up.reshape(D, 2 * FF)))
    hidden = low(jax.nn.silu(gate_values[:, :FF]) * gate_values[:, FF:])
    return middle + low_back(matmul(hidden, down_proj.T))

def reference(tokens, norm_gain, qkv_weight, heads_gain, mamba_in, conv_weight, conv_bias, state_proj, step_proj, step_bias, decay_log, skip_gain, mamba_gain, heads_out, mamba_out, mlp_gain, gate_up, down_proj, cotangent):
    inputs_full = tuple((member.astype(jnp.float32) for member in (tokens, norm_gain, qkv_weight, heads_gain, mamba_in, conv_weight, conv_bias, state_proj, step_proj, step_bias, decay_log, skip_gain, mamba_gain, heads_out, mamba_out, mlp_gain, gate_up, down_proj)))
    layer_value, pullback = jax.vjp(forward, *inputs_full)
    grads = pullback(cotangent.astype(jnp.float32))
    return (layer_value.astype(jnp.bfloat16), grads[0], grads[1], grads[2], grads[3], grads[4], grads[5], grads[6], grads[7], grads[8], grads[9], grads[10], grads[11], grads[12], grads[13], grads[14], grads[15], grads[16], grads[17])
```

```python
import functools

import jax
import jax.numpy as jnp
from jax import lax
from jax.experimental import pallas as pl
from jax.experimental.pallas import tpu as pltpu
from jax.sharding import Mesh, PartitionSpec as P

KV_HEADS = 5
GROUP = 5
HEAD = 64
INNER = 3200
STATE = 16
CONV = 4
WINDOW = 1024
STEP = 8
LANES = 128

epsilon = 1e-06


def spread(row, like):
    return jnp.broadcast_to(row, like.shape)


def column(block, index, like):
    return jnp.broadcast_to(block[:, index : index + 1], like.shape)


def turned(block, start):
    return pltpu.roll(block, lax.rem(LANES - start, LANES), 1)


def local_kernel(dt_ref, x_ref, b_ref, rate_ref, out_ref, total_ref):
    @pl.when(pl.program_id(0) == 0)
    def _():
        out_ref[...] = jnp.zeros_like(out_ref)
        total_ref[...] = jnp.zeros_like(total_ref)

    rates = rate_ref[...]
    b_all = b_ref[...]

    def block(j, carry):
        state, total = carry
        start = pl.multiple_of(j * STEP, STEP)
        dt = dt_ref[pl.ds(start, STEP), :]
        drive = dt * x_ref[pl.ds(start, STEP), :]
        b_cols = turned(b_all, start)
        for i in range(STEP):
            decay = jnp.exp(spread(dt[i : i + 1], state) * rates)
            state = decay * state + spread(drive[i : i + 1], state) * column(b_cols, i, state)
        return state, total + dt

    state, total = lax.fori_loop(
        0, dt_ref.shape[0] // STEP, block, (out_ref[...], total_ref[...])
    )
    out_ref[...] = state
    total_ref[...] = total


def value_kernel(dt_ref, x_ref, b_ref, c_ref, rate_ref, enter_ref, out_ref, state_ref):
    @pl.when(pl.program_id(0) == 0)
    def _():
        state_ref[...] = enter_ref[...]

    rates = rate_ref[...]
    b_all = b_ref[...]
    c_all = c_ref[...]

    def block(j, state):
        start = pl.multiple_of(j * STEP, STEP)
        dt = dt_ref[pl.ds(start, STEP), :]
        drive = dt * x_ref[pl.ds(start, STEP), :]
        b_cols = turned(b_all, start)
        c_cols = turned(c_all, start)
        rows = []
        for i in range(STEP):
            decay = jnp.exp(spread(dt[i : i + 1], state) * rates)
            state = decay * state + spread(drive[i : i + 1], state) * column(b_cols, i, state)
            rows.append(jnp.sum(state * column(c_cols, i, state), 0, keepdims=True))
        out_ref[pl.ds(start, STEP), :] = jnp.concatenate(rows, 0)
        return state

    state_ref[...] = lax.fori_loop(0, dt_ref.shape[0] // STEP, block, state_ref[...])


def push_kernel(dt_ref, dy_ref, c_ref, rate_ref, out_ref):
    @pl.when(pl.program_id(0) == 0)
    def _():
        out_ref[...] = jnp.zeros_like(out_ref)

    rates = rate_ref[...]
    c_all = c_ref[...]
    count = dt_ref.shape[0] // STEP

    def block(k, push):
        start = pl.multiple_of((count - 1 - k) * STEP, STEP)
        dt = dt_ref[pl.ds(start, STEP), :]
        dy = dy_ref[pl.ds(start, STEP), :]
        c_cols = turned(c_all, start)
        for i in range(STEP - 1, -1, -1):
            decay = jnp.exp(spread(dt[i : i + 1], push) * rates)
            push = decay * (push + spread(dy[i : i + 1], push) * column(c_cols, i, push))
        return push

    out_ref[...] = lax.fori_loop(0, count, block, out_ref[...])


def back_kernel(
    half,
    dt_ref,
    x_ref,
    dy_ref,
    b_ref,
    c_ref,
    rate_ref,
    enter_ref,
    future_ref,
    ddt_ref,
    dx_ref,
    db_ref,
    dc_ref,
    drate_ref,
    kept_ref,
    state_ref,
):
    step = pl.program_id(0)
    rates = rate_ref[...]
    b_all = b_ref[...]
    rows = dt_ref.shape[0]
    count = rows // STEP

    @pl.when(step == 0)
    def _():
        state_ref[...] = enter_ref[...]

    @pl.when(step < half)
    def _():
        def block(j, state):
            start = pl.multiple_of(j * STEP, STEP)
            dt = dt_ref[pl.ds(start, STEP), :]
            drive = dt * x_ref[pl.ds(start, STEP), :]
            b_cols = turned(b_all, start)
            for i in range(STEP):
                kept_ref[step * rows + start + i] = state
                decay = jnp.exp(spread(dt[i : i + 1], state) * rates)
                state = decay * state + spread(drive[i : i + 1], state) * column(b_cols, i, state)
            return state

        state_ref[...] = lax.fori_loop(0, count, block, state_ref[...])

    @pl.when(step == half)
    def _():
        state_ref[...] = future_ref[...]
        drate_ref[...] = jnp.zeros_like(drate_ref)

    @pl.when(step >= half)
    def _():
        base = (2 * half - 1 - step) * rows
        c_all = c_ref[...]
        lane = lax.broadcasted_iota(jnp.int32, b_all.shape, 1)

        def narrow(wide):
            parts = wide[:, :LANES]
            for first in range(LANES, wide.shape[1], LANES):
                parts = parts + wide[:, first : first + LANES]
            return jnp.sum(parts, 1, keepdims=True)

        def block(k, carry):
            push, drate, db, dc = carry
            start = pl.multiple_of((count - 1 - k) * STEP, STEP)
            dt = dt_ref[pl.ds(start, STEP), :]
            x = x_ref[pl.ds(start, STEP), :]
            dy = dy_ref[pl.ds(start, STEP), :]
            drive = dt * x
            b_cols = turned(b_all, start)
            c_cols = turned(c_all, start)
            first_rows = [None] * STEP
            second_rows = [None] * STEP
            for i in range(STEP - 1, -1, -1):
                before = kept_ref[base + start + i]
                dt_wide = spread(dt[i : i + 1], before)
                dy_wide = spread(dy[i : i + 1], before)
                drive_wide = spread(drive[i : i + 1], before)
                b_wide = column(b_cols, i, before)
                decay = jnp.exp(dt_wide * rates)
                moved = decay * before
                state = moved + drive_wide * b_wide
                push = push + dy_wide * column(c_cols, i, before)
                here = lane == start + i
                dc = jnp.where(here, narrow(dy_wide * state), dc)
                db = jnp.where(here, narrow(push * drive_wide), db)
                mixed = push * moved
                drate = drate + dt_wide * mixed
                first_rows[i] = jnp.sum(rates * mixed, 0, keepdims=True)
                second_rows[i] = jnp.sum(push * b_wide, 0, keepdims=True)
                push = decay * push
            second = jnp.concatenate(second_rows, 0)
            ddt_ref[pl.ds(start, STEP), :] = jnp.concatenate(first_rows, 0) + x * second
            dx_ref[pl.ds(start, STEP), :] = dt * second
            return push, drate, db, dc

        zero = jnp.zeros(b_all.shape, jnp.float32)
        push, drate, db, dc = lax.fori_loop(
            0, count, block, (state_ref[...], drate_ref[...], zero, zero)
        )
        state_ref[...] = push
        drate_ref[...] = drate
        db_ref[...] = db
        dc_ref[...] = dc


def whole(shape):
    return pl.BlockSpec(shape, lambda s: (0,) * len(shape))


def params():
    return pltpu.CompilerParams(
        dimension_semantics=("arbitrary",), vmem_limit_bytes=48 * 1024 * 1024
    )


def cost(rows, width, states, ops):
    return pl.CostEstimate(
        flops=rows * width * states * ops,
        bytes_accessed=rows * width * 16,
        transcendentals=rows * width * states,
    )


def local_scan(dt, x, b_t, rates):
    rows, width = dt.shape
    states = rates.shape[0]
    by_row = pl.BlockSpec((LANES, width), lambda s: (s, 0))
    by_lane = pl.BlockSpec((states, LANES), lambda s: (0, s))
    state, total = pl.pallas_call(
        local_kernel,
        grid=(rows // LANES,),
        in_specs=[by_row, by_row, by_lane, whole((states, width))],
        out_specs=[whole((states, width)), whole((STEP, width))],
        out_shape=[
            jax.ShapeDtypeStruct((states, width), jnp.float32),
            jax.ShapeDtypeStruct((STEP, width), jnp.float32),
        ],
        compiler_params=params(),
        cost_estimate=cost(rows, width, states, 6),
        name="scan_local",
    )(dt, x, b_t, rates)
    return state, jnp.sum(total, 0, keepdims=True)


def value_scan(dt, x, b_t, c_t, rates, entering):
    rows, width = dt.shape
    states = rates.shape[0]
    by_row = pl.BlockSpec((LANES, width), lambda s: (s, 0))
    by_lane = pl.BlockSpec((states, LANES), lambda s: (0, s))
    wide = whole((states, width))
    return pl.pallas_call(
        value_kernel,
        grid=(rows // LANES,),
        in_specs=[by_row, by_row, by_lane, by_lane, wide, wide],
        out_specs=by_row,
        out_shape=jax.ShapeDtypeStruct((rows, width), jnp.float32),
        scratch_shapes=[pltpu.VMEM((states, width), jnp.float32)],
        compiler_params=params(),
        cost_estimate=cost(rows, width, states, 8),
        name="scan_value",
    )(dt, x, b_t, c_t, rates, entering)


def push_scan(dt, dy, c_t, rates):
    rows, width = dt.shape
    states = rates.shape[0]
    last = rows // LANES - 1
    by_row = pl.BlockSpec((LANES, width), lambda s: (last - s, 0))
    by_lane = pl.BlockSpec((states, LANES), lambda s: (0, last - s))
    wide = whole((states, width))
    return pl.pallas_call(
        push_kernel,
        grid=(rows // LANES,),
        in_specs=[by_row, by_row, by_lane, wide],
        out_specs=wide,
        out_shape=jax.ShapeDtypeStruct((states, width), jnp.float32),
        compiler_params=params(),
        cost_estimate=cost(rows, width, states, 6),
        name="scan_push",
    )(dt, dy, c_t, rates)


def back_scan(dt, x, dy, b_t, c_t, rates, entering, future):
    rows, width = dt.shape
    states = rates.shape[0]
    half = rows // LANES
    both = lambda s: jnp.where(s < half, s, 2 * half - 1 - s)
    late = lambda s: jnp.where(s < half, half - 1, 2 * half - 1 - s)
    row_both = pl.BlockSpec((LANES, width), lambda s: (both(s), 0))
    lane_both = pl.BlockSpec((states, LANES), lambda s: (0, both(s)))
    row_late = pl.BlockSpec((LANES, width), lambda s: (late(s), 0))
    lane_late = pl.BlockSpec((states, LANES), lambda s: (0, late(s)))
    wide = whole((states, width))
    return pl.pallas_call(
        functools.partial(back_kernel, half),
        grid=(2 * half,),
        in_specs=[row_both, row_both, row_late, lane_both, lane_late, wide, wide, wide],
        out_specs=[row_late, row_late, lane_late, lane_late, wide],
        out_shape=[
            jax.ShapeDtypeStruct((rows, width), jnp.float32),
            jax.ShapeDtypeStruct((rows, width), jnp.float32),
            jax.ShapeDtypeStruct((states, rows), jnp.float32),
            jax.ShapeDtypeStruct((states, rows), jnp.float32),
            jax.ShapeDtypeStruct((states, width), jnp.float32),
        ],
        scratch_shapes=[
            pltpu.VMEM((rows, states, width), jnp.float32),
            pltpu.VMEM((states, width), jnp.float32),
        ],
        compiler_params=params(),
        cost_estimate=cost(rows, width, states, 20),
        name="scan_back",
    )(dt, x, dy, b_t, c_t, rates, entering, future)


BLOCK = 64
PAD_ROWS = 32


def bf(value):
    return value.astype(jnp.bfloat16)


def fl(value):
    return value.astype(jnp.float32)


def dot(left, right, contract):
    return lax.dot_general(
        left, right, (contract, ((), ())), preferred_element_type=jnp.float32
    )


def mm(left, right):
    return dot(left, right, ((1,), (0,)))


def mm_t(left, right):
    return dot(left, right, ((1,), (1,)))


def t_mm(left, right):
    return dot(left, right, ((0,), (0,)))


def swap(value):
    return lax.ppermute(value, "w", [(0, 1), (1, 0)])


def pull(value, axis, amount):
    count = lax.axis_size(axis)
    return lax.ppermute(value, axis, [((i + amount) % count, i) for i in range(count)])


def around(value, axis):
    return [value] + [pull(value, axis, k) for k in range(1, lax.axis_size(axis))]


def ordered(pieces, axis):
    count = len(pieces)
    ring = jnp.stack(pieces + pieces[:-1])
    start = lax.rem(count - lax.axis_index(axis), count)
    return lax.dynamic_slice_in_dim(ring, start, count, 0)


def pick(value, index, dim):
    return lax.dynamic_index_in_dim(value, index, dim, keepdims=False)


def sum_group(value):
    value = value + swap(value)
    value = value + lax.ppermute(value, "y", [(0, 1), (1, 0), (2, 3), (3, 2)])
    return value + lax.ppermute(value, "y", [(0, 3), (3, 0), (1, 2), (2, 1)])


def finish_scatter(parts):
    total = parts[0]
    count = len(parts)
    for k in range(1, count):
        route = [(i, (i + k) % count) for i in range(count)]
        total = total + fl(lax.ppermute(bf(parts[k]), "y", route))
    return total


def scatter_near(part):
    rows, width = part.shape
    split = part.reshape(2, 4, rows // 8, width)
    summed = split[0] + fl(swap(bf(split[1])))
    return finish_scatter([summed[k] for k in range(4)])


def scatter_true(part):
    rows, width = part.shape
    mine, half = lax.axis_index("y"), lax.axis_index("w")
    split = part.reshape(4, 2, rows // 8, width)
    summed = pick(split, half, 1) + fl(swap(bf(pick(split, 1 - half, 1))))
    return finish_scatter([pick(summed, lax.rem(mine + k, 4), 0) for k in range(4)])


def gather_near(value):
    stacked = jnp.stack(around(value, "y"))
    return jnp.stack((stacked, swap(stacked))).reshape(-1, value.shape[-1])


def gather_true(value):
    stacked = ordered(around(value, "y"), "y")
    other = swap(stacked)
    first = lax.axis_index("w") == 0
    both = jnp.stack((jnp.where(first, stacked, other), jnp.where(first, other, stacked)), 1)
    return both.reshape(-1, value.shape[-1])


def by_half(own, other, dim):
    first = lax.axis_index("w") == 0
    return jnp.concatenate((jnp.where(first, own, other), jnp.where(first, other, own)), dim)


def chain(value, rates, axis, backward):
    states = rates.shape[0]
    pieces = ordered(around(value, axis), axis)
    count = pieces.shape[0]
    mine = lax.axis_index(axis)
    before = jnp.zeros_like(value)
    total = jnp.zeros_like(value)

    def join(earlier, later):
        decay = jnp.exp(rates * later[states:])
        return jnp.concatenate(
            (decay * earlier[:states] + later[:states], earlier[states:] + later[states:]), 0
        )

    for k in range(count - 1, -1, -1) if backward else range(count):
        ahead = k > mine if backward else k < mine
        before = jnp.where(ahead, join(before, pieces[k]), before)
        total = join(total, pieces[k])
    return before, total


def entering(state, steps, rates, backward):
    states = rates.shape[0]
    value = jnp.concatenate((state, steps), 0)
    near, total = chain(value, rates, "z", backward)
    far, _ = chain(total, rates, "x", backward)
    return jnp.exp(rates * near[states:]) * far[:states] + near[:states]


def from_behind(block, axes, distance):
    count = 1
    for axis in axes:
        count *= lax.axis_size(axis)
    route = [(i - distance, i) for i in range(count) if 0 <= i - distance < count]
    return lax.ppermute(block, axes, route)


def selector(width):
    place = jnp.arange(width, dtype=jnp.int32)
    block = width // BLOCK
    target = place + (PAD_ROWS - block) * (place // block)
    return bf(target[:, None] == jnp.arange(BLOCK * PAD_ROWS, dtype=jnp.int32)[None])


def pad_gain(gain):
    block = gain.shape[0] // BLOCK
    return jnp.pad(gain.reshape(BLOCK, block), ((0, 0), (0, PAD_ROWS - block))).reshape(-1)


def trim_gain(gain, width):
    return gain.reshape(BLOCK, PAD_ROWS)[:, : width // BLOCK].reshape(-1)


def trim_wide(value, chosen):
    top = lax.reduce_precision(value, 8, 7)
    return mm_t(bf(top), chosen) + mm_t(bf(value - top), chosen)


def norm_apply(values, gain):
    return values * lax.rsqrt(jnp.mean(values * values, -1, keepdims=True) + epsilon) * gain


def norm_scale(values, width):
    return lax.rsqrt(jnp.sum(values * values, -1, keepdims=True) / width + epsilon)


def norm_back(values, scale, gain, grad, width):
    pushed = grad * gain
    along = jnp.sum(pushed * values, -1, keepdims=True) / width
    return pushed * scale - values * (scale * scale * scale) * along, jnp.sum(
        grad * values * scale, 0
    )


def swiglu_gate(gate_part, up_part):
    return jax.nn.silu(gate_part) * up_part


def widen(value, dim, size):
    pads = [(0, 0)] * value.ndim
    pads[dim] = (0, size - value.shape[dim])
    return jnp.pad(value, pads)


def round_up(value, unit):
    return -(-value // unit) * unit


def chunked(weight):
    rows, parts, columns = weight.shape
    wide = round_up(columns // 4, 128)
    cut = widen(weight.reshape(rows, parts, 4, columns // 4), 3, wide)
    cut = jnp.transpose(cut, (2, 0, 1, 3)).reshape(4, rows, parts * wide)
    return widen(cut, 1, PAD_ROWS)


def unchunked(grad, rows, parts, columns):
    wide = grad.shape[2] // parts
    cut = grad[:, :rows].reshape(4, rows, parts, wide)[..., : columns // 4]
    return fl(jnp.transpose(cut, (1, 2, 0, 3)).reshape(rows, parts, columns))


def to_chunks(packed):
    moved = lax.all_to_all(packed, "y", 0, 0)
    return moved.reshape(-1, packed.shape[-1])


def gather_rows(rows):
    return lax.all_gather(rows, ("x", "z"), axis=0, tiled=True)


def settle(grad):
    rows = lax.psum_scatter(bf(grad), ("x", "z"), scatter_dimension=0, tiled=True)
    return rows.reshape(4, -1, rows.shape[-1])


def visible_mask(query_rows, key_rows, first_pos, key_first):
    query_pos = first_pos + jnp.arange(query_rows, dtype=jnp.int32)
    key_pos = key_first + jnp.arange(key_rows, dtype=jnp.int32)
    earlier = key_pos[None, :] <= query_pos[:, None]
    nearby = key_pos[None, :] > query_pos[:, None] - WINDOW
    return earlier & nearby & (key_pos[None, :] >= 0)


def head_scores(queries, keys_all, visible, score_scale):
    scores = (
        jnp.einsum("tkgd,skd->kgts", queries, keys_all, preferred_element_type=jnp.float32)
        * score_scale
    )
    return jnp.where(visible, scores, -1e30)


def attend_forward(queries, keys_all, values_all, visible, score_scale):
    scores = head_scores(queries, keys_all, visible, score_scale)
    row_max = jnp.max(scores, -1, keepdims=True)
    lifted = jnp.exp(scores - row_max)
    row_total = jnp.sum(lifted, -1, keepdims=True)
    probability = (lifted / row_total).astype(jnp.bfloat16)
    mixed_heads = jnp.einsum(
        "kgts,skd->tkgd", probability, values_all, preferred_element_type=jnp.float32
    )
    return (mixed_heads.reshape(mixed_heads.shape[0], -1), row_max + jnp.log(row_total))


def attend_backward(queries, keys_all, values_all, visible, score_scale, log_total, heads_grad):
    scores = head_scores(queries, keys_all, visible, score_scale)
    probability = jnp.where(visible, jnp.exp(scores - log_total), 0.0)
    prob_grad = jnp.einsum(
        "tkgd,skd->kgts", heads_grad, values_all, preferred_element_type=jnp.float32
    )
    row_delta = jnp.sum(probability * prob_grad, -1, keepdims=True)
    score_grad = (probability * (prob_grad - row_delta)).astype(jnp.bfloat16)
    query_grad = (
        jnp.einsum("kgts,skd->tkgd", score_grad, keys_all, preferred_element_type=jnp.float32)
        * score_scale
    )
    key_grad = (
        jnp.einsum("kgts,tkgd->skd", score_grad, queries, preferred_element_type=jnp.float32)
        * score_scale
    )
    value_grad = jnp.einsum(
        "kgts,tkgd->skd",
        probability.astype(jnp.bfloat16),
        heads_grad,
        preferred_element_type=jnp.float32,
    )
    return (query_grad, key_grad, value_grad)


def conv_apply(extended, conv_taps, conv_bias):
    tap_count = conv_taps.shape[0]
    out_rows = extended.shape[0] - tap_count + 1
    summed = conv_bias + conv_taps[0] * extended[0:out_rows]
    for offset in range(1, tap_count):
        summed = summed + conv_taps[offset] * extended[offset : offset + out_rows]
    return jax.nn.silu(summed)


def shards(
    tokens,
    norm_gain,
    qkv_weight,
    heads_gain,
    mamba_in,
    conv_weight,
    conv_bias,
    state_proj,
    step_proj,
    step_bias,
    decay_log,
    skip_gain,
    mamba_gain,
    heads_out,
    mamba_out,
    mlp_gain,
    gate_up,
    down_proj,
    cotangent,
):
    tok_rows, width = tokens.shape
    shard_rows = qkv_weight.shape[0]
    inner_half = conv_weight.shape[1]
    inner = inner_half // 4
    lanes = round_up(inner, 128)
    hidden_half = gate_up.shape[2]
    hidden = round_up(hidden_half // 4, 128)
    heads_width = KV_HEADS * GROUP * HEAD
    kv_width = KV_HEADS * HEAD
    half_width = heads_width // 2
    qkv_half = qkv_weight.shape[1] // 2
    halo_count = WINDOW // tok_rows
    score_scale = HEAD ** (-0.5)
    x_pos, z_pos = lax.axis_index("x"), lax.axis_index("z")
    y_pos, w_pos = lax.axis_index("y"), lax.axis_index("w")
    group_axes, all_axes = ("x", "z"), ("x", "z", "y")
    own_rows = tok_rows // 2
    rank = step_proj.shape[0]

    def own_half(value, dim=0):
        size = value.shape[dim] // 2
        return lax.dynamic_slice_in_dim(value, w_pos * size, size, dim)

    def own_block(value):
        return lax.dynamic_slice_in_dim(value, y_pos * tok_rows, tok_rows, 0)

    def channels(value, dim):
        part = lax.dynamic_slice_in_dim(value, y_pos * inner, inner, dim)
        return widen(fl(part), dim, lanes)

    in_full = gather_rows(to_chunks(chunked(mamba_in)))
    rest = to_chunks(
        jnp.concatenate(
            (chunked(mamba_out[:, None]), chunked(gate_up), chunked(down_proj[:, None])), 2
        )
    )
    near_rows = jnp.concatenate((own_half(qkv_weight, 1), heads_out), 1)
    near_full = lax.all_gather(
        widen(near_rows, 0, PAD_ROWS), all_axes, axis=0, tiled=True
    )
    qkv_full = near_full[:, :qkv_half]
    hout_full = near_full[:, qkv_half:]
    rest_full = gather_rows(rest)
    mout_full = rest_full[:, :lanes]
    gu_full = rest_full[:, lanes : lanes + 2 * hidden]
    down_full = rest_full[:, lanes + 2 * hidden :]

    chosen = selector(width)
    gain_first = pad_gain(norm_gain)
    gain_mid = pad_gain(mlp_gain)
    tokens_group = ordered(around(tokens, "y"), "y").reshape(4 * tok_rows, width)
    residual = mm(tokens_group, chosen)
    scale_first = norm_scale(residual, width)
    normed = bf(residual * scale_first * gain_first)
    normed_own = own_block(normed)

    mixed_in = bf(mm(normed, in_full))
    conv_in = mixed_in[:, :lanes]
    gate_float = fl(mixed_in[:, lanes:])
    tail = from_behind(conv_in[-(CONV - 1) :], group_axes, 1)
    extended = fl(jnp.concatenate((tail, conv_in), 0))
    conv_taps = channels(conv_weight, 1)
    conv_shift = channels(conv_bias, 0)
    acted_b = bf(conv_apply(extended, conv_taps, conv_shift))
    acted = fl(acted_b)
    state_weight = bf(channels(state_proj, 0))
    state_t = sum_group(dot(state_weight, acted_b, ((0,), (1,))))
    low_rank_t = bf(state_t[:rank])
    input_t = state_t[rank : rank + STATE]
    output_t = state_t[rank + STATE :]
    step_weight = bf(channels(step_proj, 1))
    step_pre = t_mm(low_rank_t, step_weight) + channels(step_bias, 0)
    steps = jax.nn.softplus(step_pre)
    rates = -jnp.exp(channels(decay_log, 0)).T
    local_state, step_total = local_scan(steps, acted, input_t, rates)
    carry_in = entering(local_state, step_total, rates, False)

    first_pos = (lax.axis_index(all_axes)) * tok_rows
    projected_half = bf(mm(normed_own, qkv_full))
    projected = by_half(projected_half, swap(projected_half), 1)
    queries = projected[:, :heads_width].reshape(tok_rows, KV_HEADS, GROUP, HEAD)
    own_pair = projected[:, heads_width:]
    sent = own_half(own_pair, 1)
    halo_half = jnp.concatenate(
        [from_behind(sent, all_axes, k) for k in range(halo_count, 0, -1)], 0
    )
    halo_pair = by_half(halo_half, swap(halo_half), 1)
    pair_all = jnp.concatenate((halo_pair, own_pair), 0)
    keys_all = pair_all[:, :kv_width].reshape(-1, KV_HEADS, HEAD)
    values_all = pair_all[:, kv_width:].reshape(-1, KV_HEADS, HEAD)
    visible = visible_mask(
        tok_rows, pair_all.shape[0], first_pos, first_pos - halo_count * tok_rows
    )
    heads_value, log_total = attend_forward(queries, keys_all, values_all, visible, score_scale)
    heads_normed = norm_apply(heads_value, heads_gain)
    heads_half = bf(own_half(heads_normed, 1))
    heads_part = mm_t(heads_half, hout_full)

    skip = channels(skip_gain, 0)
    ssm_value = value_scan(steps, acted, input_t, output_t, rates, carry_in) + skip * acted
    gate_act = jax.nn.silu(gate_float)
    gated = ssm_value * gate_act
    square_total = sum_group(jnp.sum(gated * gated, -1))
    mamba_scale = lax.rsqrt(square_total / INNER + epsilon)[:, None]
    gain_mamba = channels(mamba_gain, 0)
    mamba_normed = bf(gated * mamba_scale * gain_mamba)

    def add_block(value, block):
        held = own_block(value) + block
        return lax.dynamic_update_slice_in_dim(value, held, y_pos * tok_rows, 0)

    mixer = 0.5 * scatter_true(add_block(mm_t(mamba_normed, mout_full), heads_part))
    own_tokens = mm(own_half(tokens), chosen)
    middle = own_tokens + mixer
    scale_mid = norm_scale(middle, width)

    normed_mid = gather_near(bf(middle * scale_mid * gain_mid))
    cot_own = bf(mm(own_half(cotangent), chosen))
    cot_near = gather_near(cot_own)
    gate_values = mm(normed_mid, gu_full)
    gate_part, up_part = gate_values[:, :hidden], gate_values[:, hidden:]
    hidden_b = bf(swiglu_gate(gate_part, up_part))
    mlp = scatter_near(mm_t(hidden_b, down_full))
    out_half = bf(mm_t(bf(middle + mlp), chosen))
    layer_out = by_half(out_half, swap(out_half), 0)
    hidden_grad = mm(cot_near, down_full)
    gate_grad, up_grad = jax.vjp(swiglu_gate, gate_part, up_part)[1](hidden_grad)
    gate_values_grad = bf(jnp.concatenate((gate_grad, up_grad), 1))
    mid_grad = scatter_near(mm_t(gate_values_grad, gu_full))
    mid_back, mlp_gain_grad = norm_back(middle, scale_mid, gain_mid, mid_grad, width)
    middle_grad = fl(cot_own) + mid_back
    gu_rows = settle(t_mm(normed_mid, gate_values_grad))
    down_rows = settle(t_mm(cot_near, hidden_b))

    mixer_grad = gather_true(bf(middle_grad))
    mamba_normed_grad = 0.5 * mm(mixer_grad, mout_full)
    half_grad = 0.5 * mm(own_block(mixer_grad), hout_full)
    heads_cut = widen(heads_half.reshape(tok_rows, 4, half_width // 4), 2, 256)
    heads_chunk = to_chunks(jnp.transpose(heads_cut, (1, 0, 2)))
    out_rows = settle(
        0.5 * t_mm(mixer_grad, jnp.concatenate((mamba_normed, heads_chunk), 1))
    )
    row_total = sum_group(jnp.sum(mamba_normed_grad * gain_mamba * gated, -1))
    gated_grad = (
        mamba_normed_grad * gain_mamba * mamba_scale
        - gated * mamba_scale**3 * row_total[:, None] / INNER
    )
    mamba_gain_grad = jnp.sum(mamba_normed_grad * gated * mamba_scale, 0)
    ssm_grad = gated_grad * gate_act
    gate_in_grad = jax.vjp(jax.nn.silu, gate_float)[1](gated_grad * ssm_value)[0]
    push = push_scan(steps, ssm_grad, output_t, rates)
    future = entering(push, step_total, rates, True)

    heads_normed_grad = by_half(half_grad, swap(half_grad), 1)
    heads_value_grad, heads_gain_grad = jax.vjp(norm_apply, heads_value, heads_gain)[1](
        heads_normed_grad
    )
    heads_grad = bf(heads_value_grad).reshape(tok_rows, KV_HEADS, GROUP, HEAD)
    query_grad, key_grad, value_grad = attend_backward(
        queries, keys_all, values_all, visible, score_scale, log_total, heads_grad
    )
    key_grad = key_grad.reshape(-1, kv_width)
    value_grad = value_grad.reshape(-1, kv_width)
    pair_half = jnp.where(w_pos == 0, key_grad, value_grad)
    own_pair_grad = pair_half[halo_count * tok_rows :]
    for amount in range(halo_count, 0, -1):
        first = (halo_count - amount) * tok_rows
        own_pair_grad = own_pair_grad + fl(
            from_behind(bf(pair_half[first : first + tok_rows]), all_axes, -amount)
        )
    own_pair_grad = bf(own_pair_grad)
    projected_grad = jnp.concatenate(
        (
            bf(query_grad.reshape(tok_rows, heads_width)),
            by_half(own_pair_grad, swap(own_pair_grad), 1),
        ),
        1,
    )
    projected_grad_half = own_half(projected_grad, 1)
    heads_back = mm_t(projected_grad_half, qkv_full)
    qkv_cut = widen(projected_grad_half.reshape(tok_rows, 4, qkv_half // 4), 2, 384)
    qkv_chunk = to_chunks(jnp.transpose(qkv_cut, (1, 0, 2)))

    step_grad, acted_core_grad, input_grad_t, output_grad_t, rate_grad = back_scan(
        steps, acted, ssm_grad, input_t, output_t, rates, carry_in, future
    )
    acted_core_grad = acted_core_grad + skip * ssm_grad
    skip_grad = jnp.sum(ssm_grad * acted, 0)
    step_pre_grad = step_grad * jax.nn.sigmoid(step_pre)
    step_bias_grad = jnp.sum(step_pre_grad, 0)
    step_pre_b = bf(step_pre_grad)
    step_proj_grad = mm(low_rank_t, step_pre_b)
    low_rank_grad_t = mm_t(step_weight, step_pre_b)
    state_grad_t = bf(
        sum_group(jnp.concatenate((low_rank_grad_t, input_grad_t, output_grad_t), 0))
    )
    state_proj_grad_t = mm(state_grad_t, acted_b)
    acted_grad = acted_core_grad + dot(state_grad_t, state_weight, ((0,), (1,)))
    extended_grad, conv_weight_grad, conv_bias_grad = jax.vjp(
        conv_apply, extended, conv_taps, conv_shift
    )[1](acted_grad)
    returned = from_behind(extended_grad[: CONV - 1], group_axes, -1)
    group_rows = 4 * tok_rows
    conv_in_grad = jnp.concatenate(
        (extended_grad[CONV - 1 : group_rows], extended_grad[group_rows:] + returned), 0
    )
    mixed_in_grad = bf(jnp.concatenate((conv_in_grad, gate_in_grad), 1))
    in_rows = settle(t_mm(normed, jnp.concatenate((mixed_in_grad, qkv_chunk), 1)))
    normed_grad = scatter_true(add_block(mm_t(mixed_in_grad, in_full), heads_back))
    own_scale = own_half(own_block(scale_first))
    first_back, norm_gain_grad = norm_back(
        own_tokens, own_scale, gain_first, normed_grad, width
    )
    tokens_half = trim_wide(middle_grad + first_back, chosen)
    tokens_grad = by_half(tokens_half, swap(tokens_half), 0)

    out_moved = lax.all_to_all(
        jnp.concatenate((gu_rows, down_rows, out_rows), 2), "y", 0, 0
    )
    in_moved = lax.all_to_all(in_rows, "y", 0, 0)
    gu_settled = unchunked(out_moved[:, :, : 2 * hidden], shard_rows, 2, hidden_half)
    down_settled = unchunked(
        out_moved[:, :, 2 * hidden : 3 * hidden], shard_rows, 1, hidden_half
    )[:, 0]
    mout_settled = unchunked(
        out_moved[:, :, 3 * hidden : 3 * hidden + lanes], shard_rows, 1, inner_half
    )[:, 0]
    hout_settled = unchunked(out_moved[:, :, 3 * hidden + lanes :], shard_rows, 1, half_width)[
        :, 0
    ]
    in_settled = unchunked(in_moved[:, :, : 2 * lanes], shard_rows, 2, inner_half)
    qkv_own = unchunked(in_moved[:, :, 2 * lanes :], shard_rows, 1, qkv_half)[:, 0]
    qkv_settled = by_half(qkv_own, swap(qkv_own), 1)

    inner_rows = jnp.concatenate(
        (
            state_proj_grad_t,
            step_proj_grad,
            rate_grad * rates,
            conv_weight_grad,
            conv_bias_grad[None],
            step_bias_grad[None],
            skip_grad[None],
            mamba_gain_grad[None],
        ),
        0,
    )
    gains = jnp.concatenate(
        (norm_gain_grad, mlp_gain_grad, 0.5 * widen(heads_gain_grad, 0, BLOCK * PAD_ROWS))
    ).reshape(-1, lanes)
    gains = gains + swap(gains)
    small = lax.psum(jnp.concatenate((inner_rows, gains), 0), group_axes)
    small = lax.all_gather(small, "y", axis=0)
    gains = jnp.sum(small[:, inner_rows.shape[0] :], 0).reshape(3, -1)
    by_channel = jnp.transpose(small[:, : inner_rows.shape[0], :inner], (1, 0, 2)).reshape(
        -1, inner_half
    )
    ends = state_proj.shape[1] + rank
    last = ends + STATE + CONV
    return (
        layer_out,
        tokens_grad,
        trim_gain(gains[0], width),
        qkv_settled,
        gains[2, :heads_width],
        in_settled,
        by_channel[ends + STATE : last],
        by_channel[last],
        by_channel[: state_proj.shape[1]].T,
        by_channel[state_proj.shape[1] : ends],
        by_channel[last + 1],
        by_channel[ends : ends + STATE].T,
        by_channel[last + 2],
        by_channel[last + 3],
        hout_settled,
        mout_settled,
        trim_gain(gains[1], width),
        gu_settled,
        down_settled,
    )


def solution(mesh):
    split = Mesh(mesh.devices.reshape(4, 4, 4, 2), ("x", "z", "y", "w"))
    ctx = ("x", "z", "y")
    placed = (
        P(ctx, None),
        P(),
        P(ctx, None),
        P(),
        P(ctx, None, "w"),
        P(None, "w"),
        P("w"),
        P("w", None),
        P(None, "w"),
        P("w"),
        P("w", None),
        P("w"),
        P("w"),
        P(ctx, "w"),
        P(ctx, "w"),
        P(),
        P(ctx, None, "w"),
        P(ctx, "w"),
        P(ctx, None),
    )
    return jax.shard_map(
        shards,
        mesh=split,
        in_specs=placed,
        out_specs=(
            P(ctx, None),
            P(ctx, None),
            P(),
            P(ctx, None),
            P(),
            P(ctx, None, "w"),
            P(None, "w"),
            P("w"),
            P("w", None),
            P(None, "w"),
            P("w"),
            P("w", None),
            P("w"),
            P("w"),
            P(ctx, "w"),
            P(ctx, "w"),
            P(),
            P(ctx, None, "w"),
            P(ctx, "w"),
        ),
        check_vma=False,
    )
```

```python
import functools

import jax
import jax.numpy as jnp
from jax import lax
from jax.experimental import pallas as pl
from jax.experimental.pallas import tpu as pltpu
from jax.sharding import Mesh, PartitionSpec as P

KV_HEADS = 5
GROUP = 5
HEAD = 64
INNER = 3200
STATE = 16
CONV = 4
WINDOW = 1024
STEP = 64
CHAIN = 64
SPREAD = 32
LANES = 128
MIB = 1024 * 1024
LOG2 = 0.6931471805599453

epsilon = 1e-06


def row(ref, index, like):
    return jnp.broadcast_to(ref[pl.ds(index, 1), :], like.shape)


def column(block, index, like):
    return jnp.broadcast_to(block[:, index : index + 1], like.shape)


def turned(block, start):
    return pltpu.roll(block, lax.rem(LANES - start, LANES), 1)


def local_kernel(dt_ref, u_ref, b_ref, rate_ref, out_ref):
    @pl.when(pl.program_id(0) == 0)
    def _():
        out_ref[...] = jnp.zeros_like(out_ref)

    rates = rate_ref[...]
    b_all = b_ref[...]

    def block(j, state):
        start = pl.multiple_of(j * STEP, STEP)
        b_cols = turned(b_all, start)
        for i in range(STEP):
            decay = jnp.exp2(row(dt_ref, start + i, state) * rates)
            state = decay * state + row(u_ref, start + i, state) * column(b_cols, i, state)
        return state

    out_ref[...] = lax.fori_loop(0, dt_ref.shape[0] // STEP, block, out_ref[...])


def value_kernel(dt_ref, u_ref, b_ref, c_ref, rate_ref, enter_ref, out_ref, kept_ref, state_ref):
    @pl.when(pl.program_id(0) == 0)
    def _():
        state_ref[...] = enter_ref[...]

    rates = rate_ref[...]
    b_all = b_ref[...]
    c_all = c_ref[...]

    def block(j, state):
        start = pl.multiple_of(j * STEP, STEP)
        b_cols = turned(b_all, start)
        c_cols = turned(c_all, start)
        rows = []
        for i in range(STEP):
            kept_ref[start + i] = state
            decay = jnp.exp2(row(dt_ref, start + i, state) * rates)
            state = decay * state + row(u_ref, start + i, state) * column(b_cols, i, state)
            rows.append(jnp.sum(state * column(c_cols, i, state), 0, keepdims=True))
        out_ref[pl.ds(start, STEP), :] = jnp.concatenate(rows, 0)
        return state

    state_ref[...] = lax.fori_loop(0, dt_ref.shape[0] // STEP, block, state_ref[...])


def push_kernel(dt_ref, dy_ref, c_ref, rate_ref, out_ref):
    @pl.when(pl.program_id(0) == 0)
    def _():
        out_ref[...] = jnp.zeros_like(out_ref)

    rates = rate_ref[...]
    c_all = c_ref[...]
    count = dt_ref.shape[0] // STEP

    def block(k, push):
        start = pl.multiple_of((count - 1 - k) * STEP, STEP)
        c_cols = turned(c_all, start)
        for i in range(STEP - 1, -1, -1):
            decay = jnp.exp2(row(dt_ref, start + i, push) * rates)
            push = decay * (push + row(dy_ref, start + i, push) * column(c_cols, i, push))
        return push

    out_ref[...] = lax.fori_loop(0, count, block, out_ref[...])


def back_kernel(
    dt_ref,
    u_ref,
    dy_ref,
    b_ref,
    c_ref,
    rate_ref,
    kept_ref,
    future_ref,
    first_ref,
    second_ref,
    db_ref,
    dc_ref,
    drate_ref,
    push_ref,
    adjoint_ref,
    moved_ref,
    db_wide_ref,
    dc_wide_ref,
):
    @pl.when(pl.program_id(0) == 0)
    def _():
        push_ref[...] = future_ref[...]
        drate_ref[...] = jnp.zeros_like(drate_ref)

    rates = rate_ref[...]
    b_all = b_ref[...]
    c_all = c_ref[...]
    rows = dt_ref.shape[0]
    states = rates.shape[0]

    def chain(k, push):
        start = pl.multiple_of((rows // CHAIN - 1 - k) * CHAIN, CHAIN)
        c_cols = turned(c_all, start)
        for i in range(CHAIN - 1, -1, -1):
            decay = jnp.exp2(row(dt_ref, start + i, push) * rates)
            adjoint = push + row(dy_ref, start + i, push) * column(c_cols, i, push)
            adjoint_ref[start + i] = adjoint
            moved_ref[start + i] = decay * kept_ref[start + i]
            push = decay * adjoint
        return push

    push_ref[...] = lax.fori_loop(0, rows // CHAIN, chain, push_ref[...])

    def fold(wide):
        parts = wide[:, :LANES]
        for first in range(LANES, wide.shape[1], LANES):
            parts = parts + wide[:, first : first + LANES]
        return parts

    def spread(k, drate):
        start = pl.multiple_of(k * SPREAD, SPREAD)
        b_cols = turned(b_all, start)
        first_rows = []
        second_rows = []
        for i in range(SPREAD):
            adjoint = adjoint_ref[start + i]
            moved = moved_ref[start + i]
            u_wide = row(u_ref, start + i, moved)
            b_wide = column(b_cols, i, moved)
            dc_wide_ref[start + i] = fold(row(dy_ref, start + i, moved) * (moved + u_wide * b_wide))
            db_wide_ref[start + i] = fold(adjoint * u_wide)
            mixed = adjoint * moved
            drate = drate + row(dt_ref, start + i, moved) * mixed
            first_rows.append(jnp.sum(rates * mixed, 0, keepdims=True))
            second_rows.append(jnp.sum(adjoint * b_wide, 0, keepdims=True))
        first_ref[pl.ds(start, SPREAD), :] = jnp.concatenate(first_rows, 0)
        second_ref[pl.ds(start, SPREAD), :] = jnp.concatenate(second_rows, 0)
        return drate

    drate_ref[...] = lax.fori_loop(0, rows // SPREAD, spread, drate_ref[...])
    ones = jnp.ones((8, LANES), jnp.float32)
    for wide_ref, out_ref in ((db_wide_ref, db_ref), (dc_wide_ref, dc_ref)):
        out_ref[...] = lax.dot_general(
            ones,
            wide_ref[...].reshape(rows * states, LANES),
            (((1,), (1,)), ((), ())),
            precision=lax.Precision.HIGHEST,
            preferred_element_type=jnp.float32,
        )


def whole(shape):
    return pl.BlockSpec(shape, lambda s: (0,) * len(shape))


def params():
    return pltpu.CompilerParams(
        dimension_semantics=("arbitrary",), vmem_limit_bytes=40 * MIB
    )


def cost(rows, width, states, ops):
    return pl.CostEstimate(
        flops=rows * width * states * ops,
        bytes_accessed=rows * width * 16,
        transcendentals=rows * width * states,
    )


def real(*shape):
    return jax.ShapeDtypeStruct(shape, jnp.float32)


def local_scan(dt, u, b_t, rates):
    rows, width = dt.shape
    states = rates.shape[0]
    by_row = pl.BlockSpec((LANES, width), lambda s: (s, 0))
    by_lane = pl.BlockSpec((states, LANES), lambda s: (0, s))
    return pl.pallas_call(
        local_kernel,
        grid=(rows // LANES,),
        in_specs=[by_row, by_row, by_lane, whole((states, width))],
        out_specs=whole((states, width)),
        out_shape=real(states, width),
        compiler_params=params(),
        cost_estimate=cost(rows, width, states, 6),
        name="scan_local",
    )(dt, u, b_t, rates)


def value_scan(dt, u, b_t, c_t, rates, entering):
    rows, width = dt.shape
    states = rates.shape[0]
    by_row = pl.BlockSpec((LANES, width), lambda s: (s, 0))
    by_lane = pl.BlockSpec((states, LANES), lambda s: (0, s))
    wide = whole((states, width))
    return pl.pallas_call(
        value_kernel,
        grid=(rows // LANES,),
        in_specs=[by_row, by_row, by_lane, by_lane, wide, wide],
        out_specs=[by_row, pl.BlockSpec((LANES, states, width), lambda s: (s, 0, 0))],
        out_shape=[real(rows, width), real(rows, states, width)],
        scratch_shapes=[pltpu.VMEM((states, width), jnp.float32)],
        compiler_params=params(),
        cost_estimate=cost(rows, width, states, 8),
        name="scan_value",
    )(dt, u, b_t, c_t, rates, entering)


def push_scan(dt, dy, c_t, rates):
    rows, width = dt.shape
    states = rates.shape[0]
    last = rows // LANES - 1
    by_row = pl.BlockSpec((LANES, width), lambda s: (last - s, 0))
    by_lane = pl.BlockSpec((states, LANES), lambda s: (0, last - s))
    wide = whole((states, width))
    return pl.pallas_call(
        push_kernel,
        grid=(rows // LANES,),
        in_specs=[by_row, by_row, by_lane, wide],
        out_specs=wide,
        out_shape=real(states, width),
        compiler_params=params(),
        cost_estimate=cost(rows, width, states, 6),
        name="scan_push",
    )(dt, dy, c_t, rates)


def back_scan(dt, u, dy, b_t, c_t, rates, kept, future):
    rows, width = dt.shape
    states = rates.shape[0]
    last = rows // LANES - 1
    by_row = pl.BlockSpec((LANES, width), lambda s: (last - s, 0))
    by_lane = pl.BlockSpec((states, LANES), lambda s: (0, last - s))
    flat = pl.BlockSpec((8, LANES * states), lambda s: (0, last - s))
    held = pl.BlockSpec((LANES, states, width), lambda s: (last - s, 0, 0))
    wide = whole((states, width))
    first, second, db, dc, drate = pl.pallas_call(
        back_kernel,
        grid=(rows // LANES,),
        in_specs=[by_row, by_row, by_row, by_lane, by_lane, wide, held, wide],
        out_specs=[by_row, by_row, flat, flat, wide],
        out_shape=[
            real(rows, width),
            real(rows, width),
            real(8, rows * states),
            real(8, rows * states),
            real(states, width),
        ],
        scratch_shapes=[
            pltpu.VMEM((states, width), jnp.float32),
            pltpu.VMEM((LANES, states, width), jnp.float32),
            pltpu.VMEM((LANES, states, width), jnp.float32),
            pltpu.VMEM((LANES, states, LANES), jnp.float32),
            pltpu.VMEM((LANES, states, LANES), jnp.float32),
        ],
        compiler_params=params(),
        cost_estimate=cost(rows, width, states, 20),
        name="scan_back",
    )(dt, u, dy, b_t, c_t, rates, kept, future)
    return first, second, db[0].reshape(rows, states).T, dc[0].reshape(rows, states).T, drate

def stacked_heads(ref, head, group):
    first = head * group * HEAD
    parts = [ref[:, first + g * HEAD : first + (g + 1) * HEAD] for g in range(group)]
    return jnp.concatenate(parts, 0)


def flat_heads(value, group):
    rows = value.shape[0] // group
    return jnp.concatenate([value[g * rows : (g + 1) * rows] for g in range(group)], 1)


def over(left, right):
    return lax.dot_general(
        left, right, (((1,), (1,)), ((), ())), preferred_element_type=jnp.float32
    )


def down(left, right):
    return lax.dot_general(
        left, right, (((0,), (0,)), ((), ())), preferred_element_type=jnp.float32
    )


def biased_scores(queries, keys, bias, scale):
    scores = over(queries, keys)
    tokens = bias.shape[0]
    return (scores.reshape(-1, tokens, scores.shape[1]) * scale + bias[None]).reshape(scores.shape)


def attend_kernel(
    scale, first_ref, q_ref, mine_ref, other_ref, own_ref, bias_ref, out_ref, log_ref, all_ref
):
    bias = bias_ref[...]
    halo, width = mine_ref.shape
    half = first_ref[1]
    all_ref[half, :halo] = mine_ref[...]
    all_ref[1 - half, :halo] = other_ref[...]
    all_ref[0, halo:] = own_ref[:, :width]
    all_ref[1, halo:] = own_ref[:, width:]
    seen = pl.ds(pl.multiple_of(first_ref[0], HEAD), bias.shape[1])
    key_ref, value_ref = all_ref.at[0, seen], all_ref.at[1, seen]
    outs = []
    for head in range(KV_HEADS):
        queries = stacked_heads(q_ref, head, GROUP)
        keys = key_ref[:, head * HEAD : (head + 1) * HEAD]
        values = value_ref[:, head * HEAD : (head + 1) * HEAD]
        scores = biased_scores(queries, keys, bias, scale)
        row_max = jnp.max(scores, 1, keepdims=True)
        lifted = jnp.exp(scores - row_max)
        row_total = jnp.sum(lifted, 1, keepdims=True)
        probability = (lifted * (1.0 / row_total)).astype(jnp.bfloat16)
        outs.append(
            flat_heads(jnp.dot(probability, values, preferred_element_type=jnp.float32), GROUP)
        )
        log_ref[head] = row_max + jnp.log(row_total)
    out_ref[...] = jnp.concatenate(outs, 1)


def attend_back_kernel(
    scale, first_ref, q_ref, all_ref, bias_ref, log_ref, grad_ref, dq_ref, dpair_ref
):
    bias = bias_ref[...]
    seen = pl.ds(pl.multiple_of(first_ref[0], HEAD), bias.shape[1])
    key_ref, value_ref = all_ref.at[0, seen], all_ref.at[1, seen]
    dqs, dks, dvs = [], [], []
    for head in range(KV_HEADS):
        queries = stacked_heads(q_ref, head, GROUP)
        grad = stacked_heads(grad_ref, head, GROUP)
        keys = key_ref[:, head * HEAD : (head + 1) * HEAD]
        values = value_ref[:, head * HEAD : (head + 1) * HEAD]
        probability = jnp.exp(biased_scores(queries, keys, bias, scale) - log_ref[head])
        prob_grad = over(grad, values)
        delta = jnp.sum(probability * prob_grad, 1, keepdims=True)
        score_grad = (probability * (prob_grad - delta)).astype(jnp.bfloat16)
        dq = jnp.dot(score_grad, keys, preferred_element_type=jnp.float32) * scale
        dqs.append(flat_heads(dq, GROUP))
        dks.append(down(score_grad, queries) * scale)
        dvs.append(down(probability.astype(jnp.bfloat16), grad))
    dq_ref[...] = jnp.concatenate(dqs, 1).astype(dq_ref.dtype)
    dpair_ref[...] = jnp.zeros_like(dpair_ref)
    dpair_ref[0, seen] = jnp.concatenate(dks, 1)
    dpair_ref[1, seen] = jnp.concatenate(dvs, 1)


def attend_cost(rows, keys, products):
    return pl.CostEstimate(
        flops=2 * rows * GROUP * KV_HEADS * keys * HEAD * products,
        bytes_accessed=keys * KV_HEADS * HEAD * 12,
        transcendentals=rows * GROUP * KV_HEADS * keys,
    )


def in_smem():
    return pl.BlockSpec(memory_space=pltpu.SMEM)


def in_vmem(count):
    return [pl.BlockSpec(memory_space=pltpu.VMEM)] * count


def attend(first, queries, mine, other, own, bias, scale):
    rows, width = queries.shape
    keys = mine.shape[0] + own.shape[0]
    return pl.pallas_call(
        functools.partial(attend_kernel, scale),
        in_specs=[in_smem()] + in_vmem(5),
        out_shape=[
            real(rows, width),
            real(KV_HEADS, GROUP * rows, 1),
            jax.ShapeDtypeStruct((2, keys, KV_HEADS * HEAD), jnp.bfloat16),
        ],
        compiler_params=pltpu.CompilerParams(vmem_limit_bytes=40 * MIB),
        cost_estimate=attend_cost(rows, keys, 8),
        name="attend",
    )(first, queries, mine, other, own, bias)


def attend_back(first, queries, pair, bias, log_total, grad, scale):
    rows, width = queries.shape
    return pl.pallas_call(
        functools.partial(attend_back_kernel, scale),
        in_specs=[in_smem()] + in_vmem(5),
        out_shape=[
            jax.ShapeDtypeStruct((rows, width), jnp.bfloat16),
            real(*pair.shape),
        ],
        compiler_params=pltpu.CompilerParams(vmem_limit_bytes=40 * MIB),
        cost_estimate=attend_cost(rows, pair.shape[1], 20),
        name="attend_back",
    )(first, queries, pair, bias, log_total, grad)


def weights_kernel(first_ref, first_grad_ref, second_ref, second_grad_ref, out_ref):
    split = first_grad_ref.shape[1]
    out_ref[:, :split] = down(first_ref[...], first_grad_ref[...]).astype(out_ref.dtype)
    out_ref[:, split:] = down(second_ref[...], second_grad_ref[...]).astype(out_ref.dtype)


def weight_grads(first, first_grad, second, second_grad):
    tokens, rows = first.shape
    split, wide = first_grad.shape[1], first_grad.shape[1] + second_grad.shape[1]
    tile = 256
    by_column = pl.BlockSpec((tokens, tile), lambda s: (0, s))
    return pl.pallas_call(
        weights_kernel,
        grid=(rows // tile,),
        in_specs=[by_column, whole(first_grad.shape), by_column, whole(second_grad.shape)],
        out_specs=pl.BlockSpec((tile, wide), lambda s: (s, 0)),
        out_shape=jax.ShapeDtypeStruct((rows, wide), jnp.bfloat16),
        compiler_params=params(),
        cost_estimate=pl.CostEstimate(
            flops=2 * tokens * rows * wide,
            bytes_accessed=2 * (2 * tokens * rows + tokens * wide + rows * wide),
            transcendentals=0,
        ),
        name="weight_grads",
    )(first, first_grad, second, second_grad)


BLOCK = 64
PAD_ROWS = 32


def bf(value):
    return value.astype(jnp.bfloat16)


def fl(value):
    return value.astype(jnp.float32)


def dot(left, right, contract):
    return lax.dot_general(
        left, right, (contract, ((), ())), preferred_element_type=jnp.float32
    )


def mm(left, right):
    return dot(left, right, ((1,), (0,)))


def mm_t(left, right):
    return dot(left, right, ((1,), (1,)))


def t_mm(left, right):
    return dot(left, right, ((0,), (0,)))


def swap(value):
    return lax.ppermute(value, "w", [(0, 1), (1, 0)])


def pull(value, axis, amount):
    count = lax.axis_size(axis)
    return lax.ppermute(value, axis, [((i + amount) % count, i) for i in range(count)])


def around(value, axis):
    return [value] + [pull(value, axis, k) for k in range(1, lax.axis_size(axis))]


def ordered(pieces, axis):
    count = len(pieces)
    ring = jnp.stack(pieces + pieces[:-1])
    start = lax.rem(count - lax.axis_index(axis), count)
    return lax.dynamic_slice_in_dim(ring, start, count, 0)


def pick(value, index, dim):
    return lax.dynamic_index_in_dim(value, index, dim, keepdims=False)


def sum_group(value):
    value = value + fl(swap(bf(value)))
    sent = bf(value)
    for k in range(1, 4):
        value = value + fl(pull(sent, "y", k))
    return value


def finish_scatter(parts):
    total = parts[0]
    count = len(parts)
    for k in range(1, count):
        route = [(i, (i + k) % count) for i in range(count)]
        total = total + fl(lax.ppermute(bf(parts[k]), "y", route))
    return total


def scatter_true(part):
    rows, width = part.shape
    mine, half = lax.axis_index("y"), lax.axis_index("w")
    split = part.reshape(4, 2, rows // 8, width)
    summed = pick(split, half, 1) + fl(swap(bf(pick(split, 1 - half, 1))))
    return finish_scatter([pick(summed, lax.rem(mine + k, 4), 0) for k in range(4)])


def arrange_kernel(place_ref, own_ref, other_ref, out_ref):
    half = place_ref[1]
    out_ref[0, half] = own_ref[0]
    out_ref[0, 1 - half] = other_ref[0]


def arrange(own, other):
    count, rows, width = own.shape
    place = jnp.stack((lax.axis_index("y"), lax.axis_index("w")))
    block = pl.BlockSpec(
        (1, rows, width), lambda s, place_ref: (lax.rem(s + count - place_ref[0], count), 0, 0)
    )
    return pl.pallas_call(
        arrange_kernel,
        grid_spec=pltpu.PrefetchScalarGridSpec(
            num_scalar_prefetch=1,
            grid=(count,),
            in_specs=[block, block],
            out_specs=pl.BlockSpec((1, 2, rows, width), lambda s, place_ref: (s, 0, 0, 0)),
        ),
        out_shape=jax.ShapeDtypeStruct((count, 2, rows, width), own.dtype),
        compiler_params=params(),
        cost_estimate=pl.CostEstimate(
            flops=0, bytes_accessed=8 * count * rows * width, transcendentals=0
        ),
        name="arrange",
    )(place, own, other).reshape(-1, width)


def gather_true(value):
    stacked = jnp.stack(around(value, "y"))
    return arrange(stacked, swap(stacked))


def by_half(own, other, dim):
    first = lax.axis_index("w") == 0
    return jnp.concatenate((jnp.where(first, own, other), jnp.where(first, other, own)), dim)


def exchange(pieces, axes):
    return lax.all_to_all(pieces, axes, 0, 0)


def entering(state, steps, rates, backward):
    states = rates.shape[0]
    value = jnp.concatenate((state, steps), 0)
    count = lax.axis_size("x") * lax.axis_size("z")
    mine = lax.axis_index(("x", "z"))
    pieces = exchange(jnp.broadcast_to(value[None], (count,) + value.shape), ("x", "z"))
    before = jnp.zeros_like(state)
    for k in range(count - 1, 0, -1) if backward else range(count - 1):
        ahead = k > mine if backward else k < mine
        moved = jnp.exp(rates * pieces[k, states:]) * before + pieces[k, :states]
        before = jnp.where(ahead, moved, before)
    return before


def from_behind(block, axes, distance):
    count = 1
    for axis in axes:
        count *= lax.axis_size(axis)
    route = [(i - distance, i) for i in range(count) if 0 <= i - distance < count]
    return lax.ppermute(block, axes, route)


def from_earlier(block):
    groups = ("x", "z")
    mine = lax.axis_index("y")
    behind = from_behind(block, groups, 1)
    beyond = from_behind(block, groups, 2)
    near, far = [], []
    for k in range(1, 4):
        wraps = mine + k >= 4
        sent = jnp.concatenate(
            (jnp.where(wraps, beyond, behind), jnp.where(wraps, behind, block)), 0
        )
        got = lax.ppermute(sent, "y", [(i, (i + k) % 4) for i in range(4)])
        far.append(got[: block.shape[0]])
        near.append(got[block.shape[0] :])
    return jnp.concatenate([beyond] + far[::-1] + [behind] + near[::-1], 0)


def to_earlier(grads, rows):
    groups = ("x", "z")
    mine = lax.axis_index("y")
    block = [grads[k * rows : (k + 1) * rows] for k in range(9)]
    own, behind, beyond = block[8], block[4], block[0]
    for k in range(1, 4):
        sent = bf(jnp.concatenate((block[4 - k], block[8 - k]), 0))
        got = fl(lax.ppermute(sent, "y", [(i, (i - k) % 4) for i in range(4)]))
        far, near = got[:rows], got[rows:]
        wraps = mine + k >= 4
        own = own + jnp.where(wraps, 0.0, near)
        behind = behind + jnp.where(wraps, near, far)
        beyond = beyond + jnp.where(wraps, far, 0.0)
    return (
        own
        + fl(from_behind(bf(behind), groups, -1))
        + fl(from_behind(bf(beyond), groups, -2))
    )


def selector(width):
    place = jnp.arange(width, dtype=jnp.int32)
    block = width // BLOCK
    target = place + (PAD_ROWS - block) * (place // block)
    return bf(target[:, None] == jnp.arange(BLOCK * PAD_ROWS, dtype=jnp.int32)[None])


def pad_gain(gain):
    block = gain.shape[0] // BLOCK
    return jnp.pad(gain.reshape(BLOCK, block), ((0, 0), (0, PAD_ROWS - block))).reshape(-1)


def trim_gain(gain, width):
    return gain.reshape(BLOCK, PAD_ROWS)[:, : width // BLOCK].reshape(-1)


def trim_wide(value, chosen):
    top = lax.reduce_precision(value, 8, 7)
    return mm_t(bf(top), chosen) + mm_t(bf(value - top), chosen)


def norm_apply(values, gain):
    return values * lax.rsqrt(jnp.mean(values * values, -1, keepdims=True) + epsilon) * gain


def norm_scale(values, width):
    return lax.rsqrt(jnp.sum(values * values, -1, keepdims=True) / width + epsilon)


def norm_back(values, scale, gain, grad, width):
    pushed = grad * gain
    along = jnp.sum(pushed * values, -1, keepdims=True) / width
    return pushed * scale - values * (scale * scale * scale) * along, jnp.sum(
        grad * values * scale, 0
    )


def swiglu_gate(gate_part, up_part):
    return jax.nn.silu(gate_part) * up_part


def widen(value, dim, size):
    pads = [(0, 0)] * value.ndim
    pads[dim] = (0, size - value.shape[dim])
    return jnp.pad(value, pads)


def round_up(value, unit):
    return -(-value // unit) * unit


def chunked(weight):
    rows, parts, columns = weight.shape
    wide = round_up(columns // 4, 128)
    cut = widen(weight.reshape(rows, parts, 4, columns // 4), 3, wide)
    cut = jnp.transpose(cut, (2, 0, 1, 3)).reshape(4, rows, parts * wide)
    return widen(cut, 1, PAD_ROWS)


def unchunked(grad, rows, parts, columns):
    wide = grad.shape[2] // parts
    cut = grad[:, :rows].reshape(4, rows, parts, wide)[..., : columns // 4]
    return fl(jnp.transpose(cut, (1, 2, 0, 3)).reshape(rows, parts, columns))


def to_chunks(packed):
    moved = lax.all_to_all(packed, "y", 0, 0)
    return moved.reshape(-1, packed.shape[-1])


def gather_rows(rows):
    return lax.all_gather(rows, ("x", "z"), axis=0, tiled=True)


def settle(grad):
    rows = lax.psum_scatter(bf(grad), ("x", "z"), scatter_dimension=0, tiled=True)
    return rows.reshape(4, -1, rows.shape[-1])


def conv_apply(extended, conv_taps, conv_bias):
    tap_count = conv_taps.shape[0]
    out_rows = extended.shape[0] - tap_count + 1
    summed = conv_bias + conv_taps[0] * extended[0:out_rows]
    for offset in range(1, tap_count):
        summed = summed + conv_taps[offset] * extended[offset : offset + out_rows]
    return jax.nn.silu(summed)


def shards(
    tokens,
    norm_gain,
    qkv_weight,
    heads_gain,
    mamba_in,
    conv_weight,
    conv_bias,
    state_proj,
    step_proj,
    step_bias,
    decay_log,
    skip_gain,
    mamba_gain,
    heads_out,
    mamba_out,
    mlp_gain,
    gate_up,
    down_proj,
    cotangent,
):
    tok_rows, width = tokens.shape
    shard_rows = qkv_weight.shape[0]
    inner_half = conv_weight.shape[1]
    inner = inner_half // 4
    lanes = round_up(inner, 128)
    hidden_half = gate_up.shape[2]
    hidden = round_up(hidden_half // 4, 128)
    heads_width = KV_HEADS * GROUP * HEAD
    kv_width = KV_HEADS * HEAD
    half_width = heads_width // 2
    qkv_half = qkv_weight.shape[1] // 2
    halo_count = WINDOW // tok_rows
    score_scale = HEAD ** (-0.5)
    x_pos, z_pos = lax.axis_index("x"), lax.axis_index("z")
    y_pos, w_pos = lax.axis_index("y"), lax.axis_index("w")
    group_axes, all_axes = ("x", "z"), ("x", "z", "y")
    own_rows = tok_rows // 2
    rank = step_proj.shape[0]

    def own_half(value, dim=0):
        size = value.shape[dim] // 2
        return lax.dynamic_slice_in_dim(value, w_pos * size, size, dim)

    def other_half(value, dim=0):
        size = value.shape[dim] // 2
        return lax.dynamic_slice_in_dim(value, (1 - w_pos) * size, size, dim)

    def own_block(value):
        return lax.dynamic_slice_in_dim(value, y_pos * tok_rows, tok_rows, 0)

    def channels(value, dim):
        part = lax.dynamic_slice_in_dim(value, y_pos * inner, inner, dim)
        return widen(fl(part), dim, lanes)

    qkv_wide, hout_wide = round_up(qkv_half // 4, 128), round_up(half_width // 4, 128)
    in_wide = 2 * lanes + qkv_wide
    early_full = gather_rows(
        to_chunks(
            jnp.concatenate(
                (
                    chunked(mamba_in),
                    chunked(own_half(qkv_weight, 1)[:, None]),
                    chunked(mamba_out[:, None]),
                ),
                2,
            )
        )
    )
    hout_full = lax.all_gather(widen(heads_out, 0, PAD_ROWS), all_axes, axis=0, tiled=True)
    late_full = gather_rows(
        to_chunks(jnp.concatenate((chunked(gate_up), chunked(down_proj[:, None])), 2))
    )
    gu_full = late_full[:, : 2 * hidden]
    down_full = late_full[:, 2 * hidden :]

    def to_tokens(chunk, columns):
        moved = lax.all_to_all(chunk.reshape(4, tok_rows, -1), "y", 0, 0)
        return jnp.transpose(moved[:, :, : columns // 4], (1, 0, 2)).reshape(tok_rows, columns)

    def to_columns(parts):
        cuts = [widen(rows.reshape(tok_rows, 4, -1), 2, wide) for rows, wide in parts]
        return to_chunks(jnp.transpose(jnp.concatenate(cuts, 2), (1, 0, 2)))

    chosen = selector(width)
    gain_first = pad_gain(norm_gain)
    gain_mid = pad_gain(mlp_gain)
    tokens_group = ordered(around(tokens, "y"), "y").reshape(4 * tok_rows, width)
    residual = mm(tokens_group, chosen)
    scale_first = norm_scale(residual, width)
    normed = bf(residual * scale_first * gain_first)

    cot_own = bf(mm(own_half(cotangent), chosen))
    early_full, cot_all = lax.optimization_barrier((early_full, gather_true(cot_own)))
    in_full = early_full[:, :in_wide]
    mout_full = early_full[:, in_wide:]

    mixed_in = bf(mm(normed, in_full))
    conv_in = mixed_in[:, :lanes]
    gate_float = fl(mixed_in[:, lanes : 2 * lanes])
    tail = from_behind(conv_in[-(CONV - 1) :], group_axes, 1)
    extended = fl(jnp.concatenate((tail, conv_in), 0))
    conv_taps = channels(conv_weight, 1)
    conv_shift = channels(conv_bias, 0)
    acted_b = bf(conv_apply(extended, conv_taps, conv_shift))
    acted = fl(acted_b)
    state_weight = bf(channels(state_proj, 0))
    state_t = sum_group(dot(state_weight, acted_b, ((0,), (1,))))
    low_rank_t = bf(state_t[:rank])
    input_t = state_t[rank : rank + STATE]
    output_t = state_t[rank + STATE :]
    step_weight = bf(channels(step_proj, 1))
    step_pre = t_mm(low_rank_t, step_weight) + channels(step_bias, 0)
    steps = jax.nn.softplus(step_pre)
    rates = -jnp.exp(channels(decay_log, 0)).T
    fast_rates = rates * (1.0 / LOG2)
    drive = steps * acted
    step_total = jnp.sum(steps, 0, keepdims=True)
    local_state = local_scan(steps, drive, input_t, fast_rates)
    carry_in = entering(local_state, step_total, rates, False)

    first_pos = (lax.axis_index(all_axes)) * tok_rows
    projected_half = to_tokens(mixed_in[:, 2 * lanes :], qkv_half)
    projected = by_half(projected_half, swap(projected_half), 1)
    own_first = w_pos * own_rows
    queries = own_half(projected[:, :heads_width])
    own_pair = projected[:, heads_width:]
    sent = own_half(own_pair, 1)
    halo_half = from_earlier(sent)
    seen = WINDOW + own_rows
    key_place = jnp.arange(seen, dtype=jnp.int32)[None]
    query_place = jnp.arange(own_rows, dtype=jnp.int32)[:, None]
    visible = (
        (key_place > query_place)
        & (key_place <= query_place + WINDOW)
        & (key_place >= WINDOW - first_pos - own_first)
    )
    bias = jnp.where(visible, 0.0, -1e30).astype(jnp.float32)
    place = jnp.stack((own_first, w_pos))
    heads_value, log_total, pair_all = attend(
        place, queries, halo_half, swap(halo_half), own_pair, bias, score_scale
    )
    heads_normed = bf(norm_apply(heads_value, heads_gain))
    heads_half = by_half(own_half(heads_normed, 1), swap(other_half(heads_normed, 1)), 0)
    heads_part = mm_t(heads_half, hout_full)
    heads_mixed = own_half(heads_part) + fl(swap(bf(other_half(heads_part))))

    skip = channels(skip_gain, 0)
    scanned, kept = value_scan(steps, drive, input_t, output_t, fast_rates, carry_in)
    ssm_value = scanned + skip * acted
    gate_act = jax.nn.silu(gate_float)
    gated = ssm_value * gate_act
    gain_mamba = channels(mamba_gain, 0)
    lane = lax.broadcasted_iota(jnp.int32, (1, BLOCK * PAD_ROWS), 1)

    def tuck(value, extras):
        for k, extra in enumerate(extras):
            value = jnp.where(lane == shard_rows + k, extra, value)
        return value

    squares = jnp.sum(gated * gated, -1, keepdims=True)
    unscaled = scatter_true(tuck(mm_t(bf(gated * gain_mamba), mout_full), (squares,)))
    mamba_scale_own = lax.rsqrt(unscaled[:, shard_rows : shard_rows + 1] / INNER + epsilon)
    unscaled = jnp.where(lane == shard_rows, 0.0, unscaled)
    mixer = 0.5 * (unscaled * mamba_scale_own + heads_mixed)
    own_tokens = mm(own_half(tokens), chosen)
    middle = own_tokens + mixer
    scale_mid = norm_scale(middle, width)

    normed_mid = gather_true(bf(middle * scale_mid * gain_mid))
    gate_values = mm(normed_mid, gu_full)
    gate_part, up_part = gate_values[:, :hidden], gate_values[:, hidden:]
    hidden_b = bf(swiglu_gate(gate_part, up_part))
    mlp_part = mm_t(hidden_b, down_full)
    hidden_grad = mm(cot_all, down_full)
    gate_grad, up_grad = jax.vjp(swiglu_gate, gate_part, up_part)[1](hidden_grad)
    gate_values_grad = bf(jnp.concatenate((gate_grad, up_grad), 1))
    ffn_grad = weight_grads(normed_mid, gate_values_grad, cot_all, hidden_b)
    mid_grad = scatter_true(mm_t(gate_values_grad, gu_full))
    mid_grad, ffn_grad = lax.optimization_barrier((mid_grad, ffn_grad))
    ffn_rows = settle(ffn_grad)
    mid_back, mlp_gain_grad = norm_back(middle, scale_mid, gain_mid, mid_grad, width)
    middle_grad = fl(cot_own) + mid_back

    mixer_grad_own = bf(middle_grad)
    row_total_own = 0.5 * jnp.sum(fl(mixer_grad_own) * unscaled, -1, keepdims=True)
    extras = []
    for value in (mamba_scale_own, row_total_own):
        top = lax.reduce_precision(value, 8, 7)
        extras += [bf(top), bf(value - top)]
    mixer_grad = gather_true(tuck(mixer_grad_own, extras))
    tucked = fl(mixer_grad[:, shard_rows : shard_rows + 4])
    mamba_scale = tucked[:, 0:1] + tucked[:, 1:2]
    row_total = tucked[:, 2:3] + tucked[:, 3:4]
    mamba_normed = bf(gated * mamba_scale * gain_mamba)
    mamba_normed_grad = 0.5 * mm(mixer_grad, mout_full)
    half_grad = bf(0.5 * mm(own_block(mixer_grad), hout_full))
    gated_grad = (
        mamba_normed_grad * gain_mamba * mamba_scale
        - gated * mamba_scale**3 * row_total / INNER
    )
    mamba_gain_grad = jnp.sum(mamba_normed_grad * gated * mamba_scale, 0)
    ssm_grad = gated_grad * gate_act
    gate_in_grad = jax.vjp(jax.nn.silu, gate_float)[1](gated_grad * ssm_value)[0]
    gate_in_grad = bf(gate_in_grad)
    push = push_scan(steps, ssm_grad, output_t, fast_rates)
    future = entering(push, step_total, rates, True)

    heads_normed_grad = by_half(own_half(half_grad), swap(other_half(half_grad)), 1)
    heads_value_grad, heads_gain_grad = jax.vjp(norm_apply, heads_value, heads_gain)[1](
        fl(heads_normed_grad)
    )
    query_grad, pair_grad = attend_back(
        place, queries, pair_all, bias, log_total, bf(heads_value_grad), score_scale
    )
    pair_half = pick(pair_grad, w_pos, 0) + fl(swap(bf(pick(pair_grad, 1 - w_pos, 0))))
    own_pair_grad = to_earlier(pair_half, tok_rows)
    own_pair_grad = bf(own_pair_grad)
    projected_grad = jnp.concatenate(
        (
            by_half(query_grad, swap(query_grad), 0),
            by_half(own_pair_grad, swap(own_pair_grad), 1),
        ),
        1,
    )
    projected_grad_half = own_half(projected_grad, 1)
    both_chunks = to_columns(((heads_half, hout_wide), (projected_grad_half, qkv_wide)))
    heads_chunk, qkv_chunk = both_chunks[:, :hout_wide], both_chunks[:, hout_wide:]
    gate_qkv_grad = jnp.concatenate((gate_in_grad, qkv_chunk), 1)
    out_grad = weight_grads(
        mixer_grad,
        0.5 * jnp.concatenate((mamba_normed, heads_chunk), 1),
        normed,
        gate_qkv_grad,
    )
    mlp = lax.psum_scatter(bf(mlp_part), ("y", "w"), scatter_dimension=0, tiled=True)
    future, out_grad, ffn_rows, mlp = lax.optimization_barrier(
        (future, out_grad, ffn_rows, mlp)
    )
    out_rows = settle(out_grad)
    side_back = mm_t(gate_qkv_grad, in_full[:, lanes:])

    first_part, second_part, input_grad_t, output_grad_t, rate_grad = back_scan(
        steps, drive, ssm_grad, input_t, output_t, fast_rates, kept, future
    )
    step_grad = LOG2 * first_part + acted * second_part
    acted_core_grad = steps * second_part + skip * ssm_grad
    skip_grad = jnp.sum(ssm_grad * acted, 0)
    step_pre_grad = step_grad * jax.nn.sigmoid(step_pre)
    step_bias_grad = jnp.sum(step_pre_grad, 0)
    step_pre_b = bf(step_pre_grad)
    step_proj_grad = mm(low_rank_t, step_pre_b)
    low_rank_grad_t = mm_t(step_weight, step_pre_b)
    state_grad_t = bf(
        sum_group(jnp.concatenate((low_rank_grad_t, input_grad_t, output_grad_t), 0))
    )
    state_proj_grad_t = mm(state_grad_t, acted_b)
    acted_grad = acted_core_grad + dot(state_grad_t, state_weight, ((0,), (1,)))
    extended_grad, conv_weight_grad, conv_bias_grad = jax.vjp(
        conv_apply, extended, conv_taps, conv_shift
    )[1](acted_grad)
    returned = from_behind(extended_grad[: CONV - 1], group_axes, -1)
    group_rows = 4 * tok_rows
    conv_in_grad = jnp.concatenate(
        (extended_grad[CONV - 1 : group_rows], extended_grad[group_rows:] + returned), 0
    )
    conv_in_grad = bf(conv_in_grad)
    out_half = bf(mm_t(bf(middle + fl(mlp)), chosen))
    layer_out = by_half(out_half, swap(out_half), 0)
    inner_rows = jnp.concatenate(
        (
            state_proj_grad_t,
            step_proj_grad,
            rate_grad * rates,
            conv_weight_grad,
            conv_bias_grad[None],
            step_bias_grad[None],
            skip_grad[None],
            mamba_gain_grad[None],
        ),
        0,
    )
    wide_gain = BLOCK * PAD_ROWS
    early_gains = jnp.concatenate((mlp_gain_grad, widen(heads_gain_grad, 0, wide_gain)))
    early_gains = early_gains.reshape(-1, lanes)
    inner_end, gains_end = inner_rows.shape[0], inner_rows.shape[0] + early_gains.shape[0]
    small = jnp.concatenate((inner_rows, early_gains + swap(early_gains)), 0)
    groups = lax.axis_size("x") * lax.axis_size("z")
    share = -(-gains_end // groups)
    small = widen(bf(small), 0, share * groups).reshape(groups, share, lanes)
    conv_grad = bf(t_mm(normed, conv_in_grad)).reshape(groups, -1, lanes)
    both = exchange(jnp.concatenate((conv_grad, small), 1), group_axes)
    both = bf(jnp.sum(fl(both), 0))
    conv_rows = both[:-share]
    conv_moved = exchange(conv_rows.reshape(4, -1, lanes), "y")
    normed_grad = scatter_true(side_back + mm_t(conv_in_grad, in_full[:, :lanes]))
    normed_grad, out_rows = lax.optimization_barrier((normed_grad, out_rows))
    own_scale = own_half(own_block(scale_first))
    first_back, norm_gain_grad = norm_back(
        own_tokens, own_scale, gain_first, normed_grad, width
    )
    tokens_half = trim_wide(middle_grad + first_back, chosen)
    tokens_grad = by_half(tokens_half, swap(tokens_half), 0)

    late_gain = norm_gain_grad.reshape(-1, lanes)
    late_gain = bf(late_gain + swap(late_gain))
    shared = jnp.concatenate((both[-share:], late_gain), 0)
    shared = exchange(jnp.broadcast_to(shared[None], (groups * 4,) + shared.shape), all_axes)
    late_gain = jnp.sum(fl(shared[:, share:]), 0).reshape(-1)
    small = fl(shared[:, :share].reshape(groups, 4, share, lanes))
    small = jnp.transpose(small, (1, 0, 2, 3)).reshape(4, groups * share, lanes)
    gains = jnp.sum(small[:, inner_end:gains_end], 0).reshape(2, -1)

    out_moved = lax.all_to_all(jnp.concatenate((ffn_rows, out_rows), 2), "y", 0, 0)

    def taken(moved, first, wide, parts, columns):
        return unchunked(moved[:, :, first : first + wide], shard_rows, parts, columns)

    gu_settled = taken(out_moved, 0, 2 * hidden, 2, hidden_half)
    down_settled = taken(out_moved, 2 * hidden, hidden, 1, hidden_half)[:, 0]
    first = 3 * hidden
    mout_settled = taken(out_moved, first, lanes, 1, inner_half)[:, 0]
    hout_settled = taken(out_moved, first + lanes, hout_wide, 1, half_width)[:, 0]
    first = first + lanes + hout_wide
    gate_settled = taken(out_moved, first, lanes, 1, inner_half)
    conv_settled = taken(conv_moved, 0, lanes, 1, inner_half)
    in_settled = jnp.concatenate((conv_settled, gate_settled), 1)
    qkv_own = taken(out_moved, first + lanes, qkv_wide, 1, qkv_half)[:, 0]
    qkv_settled = by_half(qkv_own, swap(qkv_own), 1)

    by_channel = jnp.transpose(small[:, :inner_end, :inner], (1, 0, 2)).reshape(
        -1, inner_half
    )
    ends = state_proj.shape[1] + rank
    last = ends + STATE + CONV
    return (
        layer_out,
        tokens_grad,
        trim_gain(late_gain, width),
        qkv_settled,
        gains[1, :heads_width],
        in_settled,
        by_channel[ends + STATE : last],
        by_channel[last],
        by_channel[: state_proj.shape[1]].T,
        by_channel[state_proj.shape[1] : ends],
        by_channel[last + 1],
        by_channel[ends : ends + STATE].T,
        by_channel[last + 2],
        by_channel[last + 3],
        hout_settled,
        mout_settled,
        trim_gain(gains[0], width),
        gu_settled,
        down_settled,
    )


def solution(mesh):
    split = Mesh(mesh.devices.reshape(4, 4, 4, 2), ("x", "z", "y", "w"))
    ctx = ("x", "z", "y")
    placed = (
        P(ctx, None),
        P(),
        P(ctx, None),
        P(),
        P(ctx, None, "w"),
        P(None, "w"),
        P("w"),
        P("w", None),
        P(None, "w"),
        P("w"),
        P("w", None),
        P("w"),
        P("w"),
        P(ctx, "w"),
        P(ctx, "w"),
        P(),
        P(ctx, None, "w"),
        P(ctx, "w"),
        P(ctx, None),
    )
    return jax.shard_map(
        shards,
        mesh=split,
        in_specs=placed,
        out_specs=(
            P(ctx, None),
            P(ctx, None),
            P(),
            P(ctx, None),
            P(),
            P(ctx, None, "w"),
            P(None, "w"),
            P("w"),
            P("w", None),
            P(None, "w"),
            P("w"),
            P("w", None),
            P("w"),
            P("w"),
            P(ctx, "w"),
            P(ctx, "w"),
            P(),
            P(ctx, None, "w"),
            P(ctx, "w"),
        ),
        check_vma=False,
    )
```

```python
import functools

import jax
import jax.numpy as jnp
from jax import lax
from jax.experimental import pallas as pl
from jax.experimental.pallas import tpu as pltpu
from jax.sharding import Mesh, PartitionSpec as P

KV_HEADS = 5
GROUP = 5
HEAD = 64
INNER = 3200
STATE = 16
CONV = 4
WINDOW = 1024
STEP = 64
CHAIN = 64
SPREAD = 32
LANES = 128
MIB = 1024 * 1024
LOG2 = 0.6931471805599453

epsilon = 1e-06


def row(ref, index, like):
    return jnp.broadcast_to(ref[pl.ds(index, 1), :], like.shape)


def column(block, index, like):
    return jnp.broadcast_to(block[:, index : index + 1], like.shape)


def turned(block, start):
    return pltpu.roll(block, lax.rem(LANES - start, LANES), 1)


def local_kernel(dt_ref, u_ref, b_ref, rate_ref, out_ref):
    @pl.when(pl.program_id(0) == 0)
    def _():
        out_ref[...] = jnp.zeros_like(out_ref)

    rates = rate_ref[...]
    b_all = b_ref[...]

    def block(j, state):
        start = pl.multiple_of(j * STEP, STEP)
        b_cols = turned(b_all, start)
        for i in range(STEP):
            decay = jnp.exp2(row(dt_ref, start + i, state) * rates)
            state = decay * state + row(u_ref, start + i, state) * column(b_cols, i, state)
        return state

    out_ref[...] = lax.fori_loop(0, dt_ref.shape[0] // STEP, block, out_ref[...])


def value_kernel(dt_ref, u_ref, b_ref, c_ref, rate_ref, enter_ref, out_ref, kept_ref, state_ref):
    @pl.when(pl.program_id(0) == 0)
    def _():
        state_ref[...] = enter_ref[...]

    rates = rate_ref[...]
    b_all = b_ref[...]
    c_all = c_ref[...]

    def block(j, state):
        start = pl.multiple_of(j * STEP, STEP)
        b_cols = turned(b_all, start)
        c_cols = turned(c_all, start)
        rows = []
        for i in range(STEP):
            kept_ref[start + i] = state
            decay = jnp.exp2(row(dt_ref, start + i, state) * rates)
            state = decay * state + row(u_ref, start + i, state) * column(b_cols, i, state)
            rows.append(jnp.sum(state * column(c_cols, i, state), 0, keepdims=True))
        out_ref[pl.ds(start, STEP), :] = jnp.concatenate(rows, 0)
        return state

    state_ref[...] = lax.fori_loop(0, dt_ref.shape[0] // STEP, block, state_ref[...])


def push_kernel(dt_ref, dy_ref, c_ref, rate_ref, out_ref):
    @pl.when(pl.program_id(0) == 0)
    def _():
        out_ref[...] = jnp.zeros_like(out_ref)

    rates = rate_ref[...]
    c_all = c_ref[...]
    count = dt_ref.shape[0] // STEP

    def block(k, push):
        start = pl.multiple_of((count - 1 - k) * STEP, STEP)
        c_cols = turned(c_all, start)
        for i in range(STEP - 1, -1, -1):
            decay = jnp.exp2(row(dt_ref, start + i, push) * rates)
            push = decay * (push + row(dy_ref, start + i, push) * column(c_cols, i, push))
        return push

    out_ref[...] = lax.fori_loop(0, count, block, out_ref[...])


def back_kernel(
    dt_ref,
    u_ref,
    dy_ref,
    b_ref,
    c_ref,
    rate_ref,
    kept_ref,
    future_ref,
    first_ref,
    second_ref,
    db_ref,
    dc_ref,
    drate_ref,
    push_ref,
    adjoint_ref,
    moved_ref,
    db_wide_ref,
    dc_wide_ref,
):
    @pl.when(pl.program_id(0) == 0)
    def _():
        push_ref[...] = future_ref[...]
        drate_ref[...] = jnp.zeros_like(drate_ref)

    rates = rate_ref[...]
    b_all = b_ref[...]
    c_all = c_ref[...]
    rows = dt_ref.shape[0]
    states = rates.shape[0]

    def chain(k, push):
        start = pl.multiple_of((rows // CHAIN - 1 - k) * CHAIN, CHAIN)
        c_cols = turned(c_all, start)
        for i in range(CHAIN - 1, -1, -1):
            decay = jnp.exp2(row(dt_ref, start + i, push) * rates)
            adjoint = push + row(dy_ref, start + i, push) * column(c_cols, i, push)
            adjoint_ref[start + i] = adjoint
            moved_ref[start + i] = decay * kept_ref[start + i]
            push = decay * adjoint
        return push

    push_ref[...] = lax.fori_loop(0, rows // CHAIN, chain, push_ref[...])

    def fold(wide):
        parts = wide[:, :LANES]
        for first in range(LANES, wide.shape[1], LANES):
            parts = parts + wide[:, first : first + LANES]
        return parts

    def spread(k, drate):
        start = pl.multiple_of(k * SPREAD, SPREAD)
        b_cols = turned(b_all, start)
        first_rows = []
        second_rows = []
        for i in range(SPREAD):
            adjoint = adjoint_ref[start + i]
            moved = moved_ref[start + i]
            u_wide = row(u_ref, start + i, moved)
            b_wide = column(b_cols, i, moved)
            dc_wide_ref[start + i] = fold(row(dy_ref, start + i, moved) * (moved + u_wide * b_wide))
            db_wide_ref[start + i] = fold(adjoint * u_wide)
            mixed = adjoint * moved
            drate = drate + row(dt_ref, start + i, moved) * mixed
            first_rows.append(jnp.sum(rates * mixed, 0, keepdims=True))
            second_rows.append(jnp.sum(adjoint * b_wide, 0, keepdims=True))
        first_ref[pl.ds(start, SPREAD), :] = jnp.concatenate(first_rows, 0)
        second_ref[pl.ds(start, SPREAD), :] = jnp.concatenate(second_rows, 0)
        return drate

    drate_ref[...] = lax.fori_loop(0, rows // SPREAD, spread, drate_ref[...])
    ones = jnp.ones((LANES, LANES), jnp.bfloat16)
    place = lax.broadcasted_iota(jnp.int32, (rows, states, LANES), 0)
    lane = lax.broadcasted_iota(jnp.int32, (rows, states, LANES), 2)
    for wide_ref, out_ref in ((db_wide_ref, db_ref), (dc_wide_ref, dc_ref)):
        wide = wide_ref[...].reshape(rows * states, LANES)
        top = wide.astype(jnp.bfloat16)
        rest = (wide - top.astype(jnp.float32)).astype(jnp.bfloat16)
        total = jnp.dot(top, ones, preferred_element_type=jnp.float32) + jnp.dot(
            rest, ones, preferred_element_type=jnp.float32
        )
        held = jnp.where(place == lane, total.reshape(rows, states, LANES), 0.0)
        out_ref[...] = jnp.sum(held, 0)


def whole(shape):
    return pl.BlockSpec(shape, lambda s: (0,) * len(shape))


def params():
    return pltpu.CompilerParams(
        dimension_semantics=("arbitrary",), vmem_limit_bytes=40 * MIB
    )


def cost(rows, width, states, ops):
    return pl.CostEstimate(
        flops=rows * width * states * ops,
        bytes_accessed=rows * width * 16,
        transcendentals=rows * width * states,
    )


def real(*shape):
    return jax.ShapeDtypeStruct(shape, jnp.float32)


def local_scan(dt, u, b_t, rates):
    rows, width = dt.shape
    states = rates.shape[0]
    by_row = pl.BlockSpec((LANES, width), lambda s: (s, 0))
    by_lane = pl.BlockSpec((states, LANES), lambda s: (0, s))
    return pl.pallas_call(
        local_kernel,
        grid=(rows // LANES,),
        in_specs=[by_row, by_row, by_lane, whole((states, width))],
        out_specs=whole((states, width)),
        out_shape=real(states, width),
        compiler_params=params(),
        cost_estimate=cost(rows, width, states, 6),
        name="scan_local",
    )(dt, u, b_t, rates)


def value_scan(dt, u, b_t, c_t, rates, entering):
    rows, width = dt.shape
    states = rates.shape[0]
    by_row = pl.BlockSpec((LANES, width), lambda s: (s, 0))
    by_lane = pl.BlockSpec((states, LANES), lambda s: (0, s))
    wide = whole((states, width))
    return pl.pallas_call(
        value_kernel,
        grid=(rows // LANES,),
        in_specs=[by_row, by_row, by_lane, by_lane, wide, wide],
        out_specs=[by_row, pl.BlockSpec((LANES, states, width), lambda s: (s, 0, 0))],
        out_shape=[real(rows, width), real(rows, states, width)],
        scratch_shapes=[pltpu.VMEM((states, width), jnp.float32)],
        compiler_params=params(),
        cost_estimate=cost(rows, width, states, 8),
        name="scan_value",
    )(dt, u, b_t, c_t, rates, entering)


def push_scan(dt, dy, c_t, rates):
    rows, width = dt.shape
    states = rates.shape[0]
    last = rows // LANES - 1
    by_row = pl.BlockSpec((LANES, width), lambda s: (last - s, 0))
    by_lane = pl.BlockSpec((states, LANES), lambda s: (0, last - s))
    wide = whole((states, width))
    return pl.pallas_call(
        push_kernel,
        grid=(rows // LANES,),
        in_specs=[by_row, by_row, by_lane, wide],
        out_specs=wide,
        out_shape=real(states, width),
        compiler_params=params(),
        cost_estimate=cost(rows, width, states, 6),
        name="scan_push",
    )(dt, dy, c_t, rates)


def back_scan(dt, u, dy, b_t, c_t, rates, kept, future):
    rows, width = dt.shape
    states = rates.shape[0]
    last = rows // LANES - 1
    by_row = pl.BlockSpec((LANES, width), lambda s: (last - s, 0))
    by_lane = pl.BlockSpec((states, LANES), lambda s: (0, last - s))
    held = pl.BlockSpec((LANES, states, width), lambda s: (last - s, 0, 0))
    wide = whole((states, width))
    return pl.pallas_call(
        back_kernel,
        grid=(rows // LANES,),
        in_specs=[by_row, by_row, by_row, by_lane, by_lane, wide, held, wide],
        out_specs=[by_row, by_row, by_lane, by_lane, wide],
        out_shape=[
            real(rows, width),
            real(rows, width),
            real(states, rows),
            real(states, rows),
            real(states, width),
        ],
        scratch_shapes=[
            pltpu.VMEM((states, width), jnp.float32),
            pltpu.VMEM((LANES, states, width), jnp.float32),
            pltpu.VMEM((LANES, states, width), jnp.float32),
            pltpu.VMEM((LANES, states, LANES), jnp.float32),
            pltpu.VMEM((LANES, states, LANES), jnp.float32),
        ],
        compiler_params=params(),
        cost_estimate=cost(rows, width, states, 20),
        name="scan_back",
    )(dt, u, dy, b_t, c_t, rates, kept, future)

def stacked_heads(ref, head, group):
    first = head * group * HEAD
    parts = [ref[:, first + g * HEAD : first + (g + 1) * HEAD] for g in range(group)]
    return jnp.concatenate(parts, 0)


def flat_heads(value, group):
    rows = value.shape[0] // group
    return jnp.concatenate([value[g * rows : (g + 1) * rows] for g in range(group)], 1)


def over(left, right):
    return lax.dot_general(
        left, right, (((1,), (1,)), ((), ())), preferred_element_type=jnp.float32
    )


def down(left, right):
    return lax.dot_general(
        left, right, (((0,), (0,)), ((), ())), preferred_element_type=jnp.float32
    )


def biased_scores(queries, keys, bias, scale):
    scores = over(queries, keys)
    tokens = bias.shape[0]
    return (scores.reshape(-1, tokens, scores.shape[1]) * scale + bias[None]).reshape(scores.shape)


def attend_kernel(
    scale, first_ref, q_ref, mine_ref, other_ref, own_ref, bias_ref, out_ref, log_ref, all_ref
):
    bias = bias_ref[...]
    halo, width = mine_ref.shape
    half = first_ref[1]
    all_ref[half, :halo] = mine_ref[...]
    all_ref[1 - half, :halo] = other_ref[...]
    all_ref[0, halo:] = own_ref[:, :width]
    all_ref[1, halo:] = own_ref[:, width:]
    seen = pl.ds(pl.multiple_of(first_ref[0], HEAD), bias.shape[1])
    key_ref, value_ref = all_ref.at[0, seen], all_ref.at[1, seen]
    outs = []
    for head in range(KV_HEADS):
        queries = stacked_heads(q_ref, head, GROUP)
        keys = key_ref[:, head * HEAD : (head + 1) * HEAD]
        values = value_ref[:, head * HEAD : (head + 1) * HEAD]
        scores = biased_scores(queries, keys, bias, scale)
        row_max = jnp.max(scores, 1, keepdims=True)
        lifted = jnp.exp(scores - row_max)
        row_total = jnp.sum(lifted, 1, keepdims=True)
        probability = (lifted * (1.0 / row_total)).astype(jnp.bfloat16)
        outs.append(
            flat_heads(jnp.dot(probability, values, preferred_element_type=jnp.float32), GROUP)
        )
        log_ref[head] = row_max + jnp.log(row_total)
    out_ref[...] = jnp.concatenate(outs, 1)


def attend_back_kernel(
    scale, first_ref, q_ref, all_ref, bias_ref, log_ref, grad_ref, dq_ref, kept_ref, sent_ref
):
    bias = bias_ref[...]
    seen = pl.ds(pl.multiple_of(first_ref[0], HEAD), bias.shape[1])
    key_ref, value_ref = all_ref.at[0, seen], all_ref.at[1, seen]
    dqs, dks, dvs = [], [], []
    for head in range(KV_HEADS):
        queries = stacked_heads(q_ref, head, GROUP)
        grad = stacked_heads(grad_ref, head, GROUP)
        keys = key_ref[:, head * HEAD : (head + 1) * HEAD]
        values = value_ref[:, head * HEAD : (head + 1) * HEAD]
        probability = jnp.exp(biased_scores(queries, keys, bias, scale) - log_ref[head])
        prob_grad = over(grad, values)
        delta = jnp.sum(probability * prob_grad, 1, keepdims=True)
        score_grad = (probability * (prob_grad - delta)).astype(jnp.bfloat16)
        dq = jnp.dot(score_grad, keys, preferred_element_type=jnp.float32) * scale
        dqs.append(flat_heads(dq, GROUP))
        dks.append(down(score_grad, queries) * scale)
        dvs.append(down(probability.astype(jnp.bfloat16), grad))
    dq_ref[...] = jnp.concatenate(dqs, 1).astype(dq_ref.dtype)
    kept_ref[...] = jnp.zeros_like(kept_ref)
    sent_ref[...] = jnp.zeros_like(sent_ref)
    key_grad = jnp.concatenate(dks, 1).astype(kept_ref.dtype)
    value_grad = jnp.concatenate(dvs, 1).astype(kept_ref.dtype)

    @pl.when(first_ref[1] == 0)
    def _():
        kept_ref[seen] = key_grad
        sent_ref[seen] = value_grad

    @pl.when(first_ref[1] != 0)
    def _():
        kept_ref[seen] = value_grad
        sent_ref[seen] = key_grad


def attend_cost(rows, keys, products):
    return pl.CostEstimate(
        flops=2 * rows * GROUP * KV_HEADS * keys * HEAD * products,
        bytes_accessed=keys * KV_HEADS * HEAD * 12,
        transcendentals=rows * GROUP * KV_HEADS * keys,
    )


def in_smem():
    return pl.BlockSpec(memory_space=pltpu.SMEM)


def in_vmem(count):
    return [pl.BlockSpec(memory_space=pltpu.VMEM)] * count


def attend(first, queries, mine, other, own, bias, scale):
    rows, width = queries.shape
    keys = mine.shape[0] + own.shape[0]
    return pl.pallas_call(
        functools.partial(attend_kernel, scale),
        in_specs=[in_smem()] + in_vmem(5),
        out_shape=[
            real(rows, width),
            real(KV_HEADS, GROUP * rows, 1),
            jax.ShapeDtypeStruct((2, keys, KV_HEADS * HEAD), jnp.bfloat16),
        ],
        compiler_params=pltpu.CompilerParams(vmem_limit_bytes=40 * MIB),
        cost_estimate=attend_cost(rows, keys, 8),
        name="attend",
    )(first, queries, mine, other, own, bias)


def attend_back(first, queries, pair, bias, log_total, grad, scale):
    rows, width = queries.shape
    return pl.pallas_call(
        functools.partial(attend_back_kernel, scale),
        in_specs=[in_smem()] + in_vmem(5),
        out_shape=[
            jax.ShapeDtypeStruct((rows, width), jnp.bfloat16),
            jax.ShapeDtypeStruct(pair.shape[1:], jnp.bfloat16),
            jax.ShapeDtypeStruct(pair.shape[1:], jnp.bfloat16),
        ],
        compiler_params=pltpu.CompilerParams(vmem_limit_bytes=40 * MIB),
        cost_estimate=attend_cost(rows, pair.shape[1], 20),
        name="attend_back",
    )(first, queries, pair, bias, log_total, grad)


def weights_kernel(plan, *refs):
    out_ref = refs[-1]
    place = 0
    for left, right, first, columns, scale in plan:
        product = down(refs[left][...], refs[right][:, first : first + columns])
        out_ref[:, place : place + columns] = (product * scale).astype(out_ref.dtype)
        place += columns


def weight_grads(groups):
    lefts = [left for left, _, _ in groups]
    rights, plan = [], []
    for k, (_, scale, parts) in enumerate(groups):
        for right, first, columns in parts:
            plan.append((k, len(groups) + len(rights), first, columns, scale))
            rights.append(right)
    tokens, rows = lefts[0].shape
    wide = sum(part[3] for part in plan)
    tile = 256
    by_column = pl.BlockSpec((tokens, tile), lambda s: (0, s))
    return pl.pallas_call(
        functools.partial(weights_kernel, tuple(plan)),
        grid=(rows // tile,),
        in_specs=[by_column] * len(lefts) + [whole(right.shape) for right in rights],
        out_specs=pl.BlockSpec((tile, wide), lambda s: (s, 0)),
        out_shape=jax.ShapeDtypeStruct((rows, wide), jnp.bfloat16),
        compiler_params=params(),
        cost_estimate=pl.CostEstimate(
            flops=2 * tokens * rows * wide,
            bytes_accessed=2 * (2 * tokens * rows + tokens * wide + rows * wide),
            transcendentals=0,
        ),
        name="weight_grads",
    )(*lefts, *rights)


BLOCK = 64
PAD_ROWS = 32


def bf(value):
    return value.astype(jnp.bfloat16)


def fl(value):
    return value.astype(jnp.float32)


def dot(left, right, contract):
    return lax.dot_general(
        left, right, (contract, ((), ())), preferred_element_type=jnp.float32
    )


def mm(left, right):
    return dot(left, right, ((1,), (0,)))


def mm_t(left, right):
    return dot(left, right, ((1,), (1,)))


def t_mm(left, right):
    return dot(left, right, ((0,), (0,)))


def swap(value):
    return lax.ppermute(value, "w", [(0, 1), (1, 0)])


def pull(value, axis, amount):
    count = lax.axis_size(axis)
    return lax.ppermute(value, axis, [((i + amount) % count, i) for i in range(count)])


def around(value, axis):
    return [value] + [pull(value, axis, k) for k in range(1, lax.axis_size(axis))]


def ordered(pieces, axis):
    count = len(pieces)
    ring = jnp.stack(pieces + pieces[:-1])
    start = lax.rem(count - lax.axis_index(axis), count)
    return lax.dynamic_slice_in_dim(ring, start, count, 0)


def pick(value, index, dim):
    return lax.dynamic_index_in_dim(value, index, dim, keepdims=False)


def sum_group(value):
    value = value + fl(swap(bf(value)))
    sent = bf(value)
    for k in range(1, 4):
        value = value + fl(pull(sent, "y", k))
    return value


def finish_scatter(parts):
    total = parts[0]
    count = len(parts)
    for k in range(1, count):
        route = [(i, (i + k) % count) for i in range(count)]
        total = total + fl(lax.ppermute(bf(parts[k]), "y", route))
    return total


def scatter_true(part):
    rows, width = part.shape
    mine, half = lax.axis_index("y"), lax.axis_index("w")
    split = part.reshape(4, 2, rows // 8, width)
    summed = pick(split, half, 1) + fl(swap(bf(pick(split, 1 - half, 1))))
    return finish_scatter([pick(summed, lax.rem(mine + k, 4), 0) for k in range(4)])


def arrange_kernel(place_ref, own_ref, other_ref, out_ref):
    half = place_ref[1]
    out_ref[0, half] = own_ref[0]
    out_ref[0, 1 - half] = other_ref[0]


def arrange(own, other):
    count, rows, width = own.shape
    place = jnp.stack((lax.axis_index("y"), lax.axis_index("w")))
    block = pl.BlockSpec(
        (1, rows, width), lambda s, place_ref: (lax.rem(s + count - place_ref[0], count), 0, 0)
    )
    return pl.pallas_call(
        arrange_kernel,
        grid_spec=pltpu.PrefetchScalarGridSpec(
            num_scalar_prefetch=1,
            grid=(count,),
            in_specs=[block, block],
            out_specs=pl.BlockSpec((1, 2, rows, width), lambda s, place_ref: (s, 0, 0, 0)),
        ),
        out_shape=jax.ShapeDtypeStruct((count, 2, rows, width), own.dtype),
        compiler_params=params(),
        cost_estimate=pl.CostEstimate(
            flops=0, bytes_accessed=8 * count * rows * width, transcendentals=0
        ),
        name="arrange",
    )(place, own, other).reshape(-1, width)


def gather_true(value):
    stacked = jnp.stack(around(value, "y"))
    return arrange(stacked, swap(stacked))


def by_half(own, other, dim):
    first = lax.axis_index("w") == 0
    return jnp.concatenate((jnp.where(first, own, other), jnp.where(first, other, own)), dim)


def exchange(pieces, axes):
    return lax.all_to_all(pieces, axes, 0, 0)


def exchange_near(blocks):
    mine = lax.axis_index("y")
    pieces = [pick(blocks, mine, 0)]
    for k in range(1, 4):
        sent = pick(blocks, lax.rem(mine + 4 - k, 4), 0)
        pieces.append(lax.ppermute(sent, "y", [(i, (i - k) % 4) for i in range(4)]))
    return ordered(pieces, "y")


def entering(state, steps, rates, backward):
    states = rates.shape[0]
    value = jnp.concatenate((state, steps), 0)
    count = lax.axis_size("x") * lax.axis_size("z")
    mine = lax.axis_index(("x", "z"))
    pieces = exchange(jnp.broadcast_to(value[None], (count,) + value.shape), ("x", "z"))
    before = jnp.zeros_like(state)
    for k in range(count - 1, 0, -1) if backward else range(count - 1):
        ahead = k > mine if backward else k < mine
        moved = jnp.exp(rates * pieces[k, states:]) * before + pieces[k, :states]
        before = jnp.where(ahead, moved, before)
    return before


def from_behind(block, axes, distance):
    count = 1
    for axis in axes:
        count *= lax.axis_size(axis)
    route = [(i - distance, i) for i in range(count) if 0 <= i - distance < count]
    return lax.ppermute(block, axes, route)


def from_earlier(block):
    groups = ("x", "z")
    mine = lax.axis_index("y")
    behind = from_behind(block, groups, 1)
    beyond = from_behind(block, groups, 2)
    near, far = [], []
    for k in range(1, 4):
        wraps = mine + k >= 4
        sent = jnp.concatenate(
            (jnp.where(wraps, beyond, behind), jnp.where(wraps, behind, block)), 0
        )
        got = lax.ppermute(sent, "y", [(i, (i + k) % 4) for i in range(4)])
        far.append(got[: block.shape[0]])
        near.append(got[block.shape[0] :])
    return jnp.concatenate([beyond] + far[::-1] + [behind] + near[::-1], 0)


def to_earlier(grads, rows):
    groups = ("x", "z")
    mine = lax.axis_index("y")
    block = [grads[k * rows : (k + 1) * rows] for k in range(9)]
    own, behind, beyond = block[8], block[4], block[0]
    for k in range(1, 4):
        sent = bf(jnp.concatenate((block[4 - k], block[8 - k]), 0))
        got = fl(lax.ppermute(sent, "y", [(i, (i - k) % 4) for i in range(4)]))
        far, near = got[:rows], got[rows:]
        wraps = mine + k >= 4
        own = own + jnp.where(wraps, 0.0, near)
        behind = behind + jnp.where(wraps, near, far)
        beyond = beyond + jnp.where(wraps, far, 0.0)
    return (
        own
        + fl(from_behind(bf(behind), groups, -1))
        + fl(from_behind(bf(beyond), groups, -2))
    )


def selector(width):
    place = jnp.arange(width, dtype=jnp.int32)
    block = width // BLOCK
    target = place + (PAD_ROWS - block) * (place // block)
    return bf(target[:, None] == jnp.arange(BLOCK * PAD_ROWS, dtype=jnp.int32)[None])


def pad_gain(gain):
    block = gain.shape[0] // BLOCK
    return jnp.pad(gain.reshape(BLOCK, block), ((0, 0), (0, PAD_ROWS - block))).reshape(-1)


def trim_gain(gain, width):
    return gain.reshape(BLOCK, PAD_ROWS)[:, : width // BLOCK].reshape(-1)


def trim_wide(value, chosen):
    top = lax.reduce_precision(value, 8, 7)
    return mm_t(bf(top), chosen) + mm_t(bf(value - top), chosen)


def norm_apply(values, gain):
    return values * lax.rsqrt(jnp.mean(values * values, -1, keepdims=True) + epsilon) * gain


def norm_scale(values, width):
    return lax.rsqrt(jnp.sum(values * values, -1, keepdims=True) / width + epsilon)


def norm_back(values, scale, gain, grad, width):
    pushed = grad * gain
    along = jnp.sum(pushed * values, -1, keepdims=True) / width
    return pushed * scale - values * (scale * scale * scale) * along, jnp.sum(
        grad * values * scale, 0
    )


def swiglu_gate(gate_part, up_part):
    return jax.nn.silu(gate_part) * up_part


def widen(value, dim, size):
    pads = [(0, 0)] * value.ndim
    pads[dim] = (0, size - value.shape[dim])
    return jnp.pad(value, pads)


def round_up(value, unit):
    return -(-value // unit) * unit


def chunked(weight):
    rows, parts, columns = weight.shape
    wide = round_up(columns // 4, 128)
    cut = widen(weight.reshape(rows, parts, 4, columns // 4), 3, wide)
    cut = jnp.transpose(cut, (2, 0, 1, 3)).reshape(4, rows, parts * wide)
    return widen(cut, 1, PAD_ROWS)


def unchunked(grad, rows, parts, columns):
    wide = grad.shape[2] // parts
    cut = grad[:, :rows].reshape(4, rows, parts, wide)[..., : columns // 4]
    return fl(jnp.transpose(cut, (1, 2, 0, 3)).reshape(rows, parts, columns))


def to_chunks(packed):
    moved = lax.all_to_all(packed, "y", 0, 0)
    return moved.reshape(-1, packed.shape[-1])


def gather_rows(rows):
    return lax.all_gather(rows, ("x", "z"), axis=0, tiled=True)


def settle(grad):
    rows = lax.psum_scatter(bf(grad), ("x", "z"), scatter_dimension=0, tiled=True)
    return rows.reshape(4, -1, rows.shape[-1])


def conv_apply(extended, conv_taps, conv_bias):
    tap_count = conv_taps.shape[0]
    out_rows = extended.shape[0] - tap_count + 1
    summed = conv_bias + conv_taps[0] * extended[0:out_rows]
    for offset in range(1, tap_count):
        summed = summed + conv_taps[offset] * extended[offset : offset + out_rows]
    return jax.nn.silu(summed)


def shards(
    tokens,
    norm_gain,
    qkv_weight,
    heads_gain,
    mamba_in,
    conv_weight,
    conv_bias,
    state_proj,
    step_proj,
    step_bias,
    decay_log,
    skip_gain,
    mamba_gain,
    heads_out,
    mamba_out,
    mlp_gain,
    gate_up,
    down_proj,
    cotangent,
):
    tok_rows, width = tokens.shape
    shard_rows = qkv_weight.shape[0]
    inner_half = conv_weight.shape[1]
    inner = inner_half // 4
    lanes = round_up(inner, 128)
    hidden_half = gate_up.shape[2]
    hidden = round_up(hidden_half // 4, 128)
    heads_width = KV_HEADS * GROUP * HEAD
    kv_width = KV_HEADS * HEAD
    half_width = heads_width // 2
    qkv_half = qkv_weight.shape[1] // 2
    halo_count = WINDOW // tok_rows
    score_scale = HEAD ** (-0.5)
    x_pos, z_pos = lax.axis_index("x"), lax.axis_index("z")
    y_pos, w_pos = lax.axis_index("y"), lax.axis_index("w")
    group_axes, all_axes = ("x", "z"), ("x", "z", "y")
    own_rows = tok_rows // 2
    rank = step_proj.shape[0]

    def own_half(value, dim=0):
        size = value.shape[dim] // 2
        return lax.dynamic_slice_in_dim(value, w_pos * size, size, dim)

    def other_half(value, dim=0):
        size = value.shape[dim] // 2
        return lax.dynamic_slice_in_dim(value, (1 - w_pos) * size, size, dim)

    def own_block(value):
        return lax.dynamic_slice_in_dim(value, y_pos * tok_rows, tok_rows, 0)

    def channels(value, dim):
        part = lax.dynamic_slice_in_dim(value, y_pos * inner, inner, dim)
        return widen(fl(part), dim, lanes)

    qkv_wide, hout_wide = round_up(qkv_half // 4, 128), round_up(half_width // 4, 128)
    in_wide = 2 * lanes + qkv_wide
    early_full = gather_rows(
        to_chunks(
            jnp.concatenate(
                (
                    chunked(mamba_in),
                    chunked(own_half(qkv_weight, 1)[:, None]),
                    chunked(mamba_out[:, None]),
                ),
                2,
            )
        )
    )
    hout_full = lax.all_gather(widen(heads_out, 0, PAD_ROWS), all_axes, axis=0, tiled=True)
    late_full = gather_rows(
        to_chunks(jnp.concatenate((chunked(gate_up), chunked(down_proj[:, None])), 2))
    )
    gu_full = late_full[:, : 2 * hidden]
    down_full = late_full[:, 2 * hidden :]

    def to_tokens(chunk, columns):
        moved = lax.all_to_all(chunk.reshape(4, tok_rows, -1), "y", 0, 0)
        return jnp.transpose(moved[:, :, : columns // 4], (1, 0, 2)).reshape(tok_rows, columns)

    def to_columns(parts):
        cuts = [widen(rows.reshape(tok_rows, 4, -1), 2, wide) for rows, wide in parts]
        return to_chunks(jnp.transpose(jnp.concatenate(cuts, 2), (1, 0, 2)))

    chosen = selector(width)
    gain_first = pad_gain(norm_gain)
    gain_mid = pad_gain(mlp_gain)
    tokens_group = ordered(around(tokens, "y"), "y").reshape(4 * tok_rows, width)
    residual = mm(tokens_group, chosen)
    scale_first = norm_scale(residual, width)
    normed = bf(residual * scale_first * gain_first)

    cot_own = bf(mm(own_half(cotangent), chosen))
    early_full, cot_all = lax.optimization_barrier((early_full, gather_true(cot_own)))
    in_full = early_full[:, :in_wide]
    mout_full = early_full[:, in_wide:]

    mixed_in = bf(mm(normed, in_full))
    conv_in = mixed_in[:, :lanes]
    gate_float = fl(mixed_in[:, lanes : 2 * lanes])
    tail = from_behind(conv_in[-(CONV - 1) :], group_axes, 1)
    extended = fl(jnp.concatenate((tail, conv_in), 0))
    conv_taps = channels(conv_weight, 1)
    conv_shift = channels(conv_bias, 0)
    acted_b = bf(conv_apply(extended, conv_taps, conv_shift))
    acted = fl(acted_b)
    state_weight = bf(channels(state_proj, 0))
    state_t = sum_group(dot(state_weight, acted_b, ((0,), (1,))))
    low_rank_t = bf(state_t[:rank])
    input_t = state_t[rank : rank + STATE]
    output_t = state_t[rank + STATE :]
    step_weight = bf(channels(step_proj, 1))
    step_pre = t_mm(low_rank_t, step_weight) + channels(step_bias, 0)
    steps = jax.nn.softplus(step_pre)
    rates = -jnp.exp(channels(decay_log, 0)).T
    fast_rates = rates * (1.0 / LOG2)
    drive = steps * acted
    step_total = jnp.sum(steps, 0, keepdims=True)
    local_state = local_scan(steps, drive, input_t, fast_rates)
    carry_in = entering(local_state, step_total, rates, False)

    first_pos = (lax.axis_index(all_axes)) * tok_rows
    projected_half = to_tokens(mixed_in[:, 2 * lanes :], qkv_half)
    projected = by_half(projected_half, swap(projected_half), 1)
    own_first = w_pos * own_rows
    queries = own_half(projected[:, :heads_width])
    own_pair = projected[:, heads_width:]
    sent = own_half(own_pair, 1)
    halo_half = from_earlier(sent)
    seen = WINDOW + own_rows
    key_place = jnp.arange(seen, dtype=jnp.int32)[None]
    query_place = jnp.arange(own_rows, dtype=jnp.int32)[:, None]
    visible = (
        (key_place > query_place)
        & (key_place <= query_place + WINDOW)
        & (key_place >= WINDOW - first_pos - own_first)
    )
    bias = jnp.where(visible, 0.0, -1e30).astype(jnp.float32)
    place = jnp.stack((own_first, w_pos))
    heads_value, log_total, pair_all = attend(
        place, queries, halo_half, swap(halo_half), own_pair, bias, score_scale
    )
    heads_normed = bf(norm_apply(heads_value, heads_gain))
    heads_half = by_half(own_half(heads_normed, 1), swap(other_half(heads_normed, 1)), 0)
    heads_part = mm_t(heads_half, hout_full)
    heads_mixed = own_half(heads_part) + fl(swap(bf(other_half(heads_part))))

    skip = channels(skip_gain, 0)
    scanned, kept = value_scan(steps, drive, input_t, output_t, fast_rates, carry_in)
    ssm_value = scanned + skip * acted
    gate_act = jax.nn.silu(gate_float)
    gated = ssm_value * gate_act
    gain_mamba = channels(mamba_gain, 0)
    lane = lax.broadcasted_iota(jnp.int32, (1, BLOCK * PAD_ROWS), 1)

    def tuck(value, extras):
        for k, extra in enumerate(extras):
            value = jnp.where(lane == shard_rows + k, extra, value)
        return value

    squares = jnp.sum(gated * gated, -1, keepdims=True)
    unscaled = scatter_true(tuck(mm_t(bf(gated * gain_mamba), mout_full), (squares,)))
    mamba_scale_own = lax.rsqrt(unscaled[:, shard_rows : shard_rows + 1] / INNER + epsilon)
    unscaled = jnp.where(lane == shard_rows, 0.0, unscaled)
    mixer = 0.5 * (unscaled * mamba_scale_own + heads_mixed)
    own_tokens = mm(own_half(tokens), chosen)
    middle = own_tokens + mixer
    scale_mid = norm_scale(middle, width)

    normed_mid = gather_true(bf(middle * scale_mid * gain_mid))
    gate_values = mm(normed_mid, gu_full)
    gate_part, up_part = gate_values[:, :hidden], gate_values[:, hidden:]
    hidden_b = bf(swiglu_gate(gate_part, up_part))
    mlp_part = mm_t(hidden_b, down_full)
    hidden_grad = mm(cot_all, down_full)
    gate_grad, up_grad = jax.vjp(swiglu_gate, gate_part, up_part)[1](hidden_grad)
    gate_values_grad = bf(jnp.concatenate((gate_grad, up_grad), 1))
    ffn_grad = weight_grads(
        (
            (normed_mid, 1.0, ((gate_values_grad, 0, 2 * hidden),)),
            (cot_all, 1.0, ((hidden_b, 0, hidden),)),
        )
    )
    mid_grad = scatter_true(mm_t(gate_values_grad, gu_full))
    mid_grad, ffn_grad = lax.optimization_barrier((mid_grad, ffn_grad))
    ffn_rows = settle(ffn_grad)
    mid_back, mlp_gain_grad = norm_back(middle, scale_mid, gain_mid, mid_grad, width)
    middle_grad = fl(cot_own) + mid_back

    mixer_grad_own = bf(middle_grad)
    row_total_own = 0.5 * jnp.sum(fl(mixer_grad_own) * unscaled, -1, keepdims=True)
    extras = []
    for value in (mamba_scale_own, row_total_own):
        top = lax.reduce_precision(value, 8, 7)
        extras += [bf(top), bf(value - top)]
    mixer_grad = gather_true(tuck(mixer_grad_own, extras))
    tucked = fl(mixer_grad[:, shard_rows : shard_rows + 4])
    mamba_scale = tucked[:, 0:1] + tucked[:, 1:2]
    row_total = tucked[:, 2:3] + tucked[:, 3:4]
    mamba_normed = bf(gated * mamba_scale * gain_mamba)
    mamba_normed_grad = 0.5 * mm(mixer_grad, mout_full)
    half_grad = bf(0.5 * mm(own_block(mixer_grad), hout_full))
    gated_grad = (
        mamba_normed_grad * gain_mamba * mamba_scale
        - gated * mamba_scale**3 * row_total / INNER
    )
    mamba_gain_grad = jnp.sum(mamba_normed_grad * gated * mamba_scale, 0)
    ssm_grad = gated_grad * gate_act
    gate_in_grad = jax.vjp(jax.nn.silu, gate_float)[1](gated_grad * ssm_value)[0]
    gate_in_grad = bf(gate_in_grad)
    push = push_scan(steps, ssm_grad, output_t, fast_rates)
    push, half_grad = lax.optimization_barrier((push, half_grad))
    future = entering(push, step_total, rates, True)

    heads_normed_grad = by_half(own_half(half_grad), swap(other_half(half_grad)), 1)
    heads_value_grad, heads_gain_grad = jax.vjp(norm_apply, heads_value, heads_gain)[1](
        fl(heads_normed_grad)
    )
    query_grad, kept_grad, sent_grad = attend_back(
        place, queries, pair_all, bias, log_total, bf(heads_value_grad), score_scale
    )
    pair_half = fl(kept_grad) + fl(swap(sent_grad))
    own_pair_grad = to_earlier(pair_half, tok_rows)
    own_pair_grad = bf(own_pair_grad)
    projected_grad = jnp.concatenate(
        (
            by_half(query_grad, swap(query_grad), 0),
            by_half(own_pair_grad, swap(own_pair_grad), 1),
        ),
        1,
    )
    projected_grad_half = own_half(projected_grad, 1)
    both_chunks = to_columns(((heads_half, hout_wide), (projected_grad_half, qkv_wide)))
    out_grad = weight_grads(
        (
            (mixer_grad, 0.5, ((mamba_normed, 0, lanes), (both_chunks, 0, hout_wide))),
            (normed, 1.0, ((gate_in_grad, 0, lanes), (both_chunks, hout_wide, qkv_wide))),
        )
    )
    mlp = lax.psum_scatter(bf(mlp_part), ("y", "w"), scatter_dimension=0, tiled=True)
    future, out_grad, ffn_rows, mlp = lax.optimization_barrier(
        (future, out_grad, ffn_rows, mlp)
    )
    out_rows = settle(out_grad)

    first_part, second_part, input_grad_t, output_grad_t, rate_grad = back_scan(
        steps, drive, ssm_grad, input_t, output_t, fast_rates, kept, future
    )
    step_grad = LOG2 * first_part + acted * second_part
    acted_core_grad = steps * second_part + skip * ssm_grad
    skip_grad = jnp.sum(ssm_grad * acted, 0)
    step_pre_grad = step_grad * jax.nn.sigmoid(step_pre)
    step_bias_grad = jnp.sum(step_pre_grad, 0)
    step_pre_b = bf(step_pre_grad)
    step_proj_grad = mm(low_rank_t, step_pre_b)
    low_rank_grad_t = mm_t(step_weight, step_pre_b)
    state_grad_t = bf(
        sum_group(jnp.concatenate((low_rank_grad_t, input_grad_t, output_grad_t), 0))
    )
    state_proj_grad_t = mm(state_grad_t, acted_b)
    acted_grad = acted_core_grad + dot(state_grad_t, state_weight, ((0,), (1,)))
    extended_grad, conv_weight_grad, conv_bias_grad = jax.vjp(
        conv_apply, extended, conv_taps, conv_shift
    )[1](acted_grad)
    returned = from_behind(extended_grad[: CONV - 1], group_axes, -1)
    group_rows = 4 * tok_rows
    conv_in_grad = jnp.concatenate(
        (extended_grad[CONV - 1 : group_rows], extended_grad[group_rows:] + returned), 0
    )
    conv_in_grad = bf(conv_in_grad)
    out_half = bf(mm_t(bf(middle + fl(mlp)), chosen))
    layer_out = by_half(out_half, swap(out_half), 0)
    wide_gain = BLOCK * PAD_ROWS
    early_gains = jnp.concatenate((mlp_gain_grad, widen(heads_gain_grad, 0, wide_gain)))
    early_gains = early_gains.reshape(-1, lanes)
    early_gains = early_gains + swap(early_gains)
    groups = lax.axis_size("x") * lax.axis_size("z")
    inner_rows = jnp.concatenate(
        (
            rate_grad * rates,
            state_proj_grad_t,
            conv_weight_grad,
            step_proj_grad,
            conv_bias_grad[None],
            step_bias_grad[None],
            skip_grad[None],
            mamba_gain_grad[None],
        ),
        0,
    )
    share = -(-inner_rows.shape[0] // groups)
    small = jnp.concatenate(
        (
            bf(widen(inner_rows, 0, share * groups)).reshape(groups, share, lanes),
            bf(widen(early_gains, 0, groups))[:, None],
        ),
        1,
    )
    conv_grad = bf(t_mm(normed, conv_in_grad)).reshape(groups, -1, lanes)
    share = small.shape[1]
    sent, conv_in_grad = lax.optimization_barrier(
        (jnp.concatenate((conv_grad, small), 1), conv_in_grad)
    )
    both = bf(jnp.sum(fl(exchange(sent, group_axes)), 0))
    conv_rows, small = both[:-share], both[-share:]
    back_grad = jnp.concatenate((conv_in_grad, gate_in_grad, both_chunks[:, hout_wide:]), 1)
    normed_grad = scatter_true(mm_t(back_grad, in_full))
    normed_grad, out_rows = lax.optimization_barrier((normed_grad, out_rows))
    own_scale = own_half(own_block(scale_first))
    first_back, norm_gain_grad = norm_back(
        own_tokens, own_scale, gain_first, normed_grad, width
    )
    tokens_half = trim_wide(middle_grad + first_back, chosen)
    tokens_grad = by_half(tokens_half, swap(tokens_half), 0)

    def to_all(rows):
        every = (groups * lax.axis_size("y"),)
        return exchange(jnp.broadcast_to(rows[None], every + rows.shape), all_axes)

    late_gain = norm_gain_grad.reshape(-1, lanes)
    late_gain = bf(late_gain + swap(late_gain))
    shared = to_all(jnp.concatenate((small, late_gain), 0))
    conv_moved = exchange_near(conv_rows.reshape(4, -1, lanes))
    out_moved = exchange_near(jnp.concatenate((ffn_rows, out_rows), 2))
    late_gain = jnp.sum(fl(shared[:, share:]), 0).reshape(-1)
    small = shared[:, :share].reshape(groups, -1, share, lanes)
    gains = jnp.sum(fl(small[: early_gains.shape[0], :, -1]), 1).reshape(2, -1)


    def taken(moved, first, wide, parts, columns):
        return unchunked(moved[:, :, first : first + wide], shard_rows, parts, columns)

    gu_settled = taken(out_moved, 0, 2 * hidden, 2, hidden_half)
    down_settled = taken(out_moved, 2 * hidden, hidden, 1, hidden_half)[:, 0]
    first = 3 * hidden
    mout_settled = taken(out_moved, first, lanes, 1, inner_half)[:, 0]
    hout_settled = taken(out_moved, first + lanes, hout_wide, 1, half_width)[:, 0]
    first = first + lanes + hout_wide
    gate_settled = taken(out_moved, first, lanes, 1, inner_half)
    conv_settled = taken(conv_moved, 0, lanes, 1, inner_half)
    in_settled = jnp.concatenate((conv_settled, gate_settled), 1)
    qkv_own = taken(out_moved, first + lanes, qkv_wide, 1, qkv_half)[:, 0]
    qkv_settled = by_half(qkv_own, swap(qkv_own), 1)

    by_channel = jnp.transpose(small[:, :, :-1, :inner], (0, 2, 1, 3)).reshape(-1, inner_half)
    by_channel = fl(by_channel)
    states_end = STATE + state_proj.shape[1]
    taps_end = states_end + CONV
    last = taps_end + rank
    return (
        layer_out,
        tokens_grad,
        trim_gain(late_gain, width),
        qkv_settled,
        gains[1, :heads_width],
        in_settled,
        by_channel[states_end:taps_end],
        by_channel[last],
        by_channel[STATE:states_end].T,
        by_channel[taps_end:last],
        by_channel[last + 1],
        by_channel[:STATE].T,
        by_channel[last + 2],
        by_channel[last + 3],
        hout_settled,
        mout_settled,
        trim_gain(gains[0], width),
        gu_settled,
        down_settled,
    )


def solution(mesh):
    split = Mesh(mesh.devices.reshape(4, 4, 4, 2), ("x", "z", "y", "w"))
    ctx = ("x", "z", "y")
    placed = (
        P(ctx, None),
        P(),
        P(ctx, None),
        P(),
        P(ctx, None, "w"),
        P(None, "w"),
        P("w"),
        P("w", None),
        P(None, "w"),
        P("w"),
        P("w", None),
        P("w"),
        P("w"),
        P(ctx, "w"),
        P(ctx, "w"),
        P(),
        P(ctx, None, "w"),
        P(ctx, "w"),
        P(ctx, None),
    )
    return jax.shard_map(
        shards,
        mesh=split,
        in_specs=placed,
        out_specs=(
            P(ctx, None),
            P(ctx, None),
            P(),
            P(ctx, None),
            P(),
            P(ctx, None, "w"),
            P(None, "w"),
            P("w"),
            P("w", None),
            P(None, "w"),
            P("w"),
            P("w", None),
            P("w"),
            P("w"),
            P(ctx, "w"),
            P(ctx, "w"),
            P(),
            P(ctx, None, "w"),
            P(ctx, "w"),
        ),
        check_vma=False,
    )
```

```python
import functools

import jax
import jax.numpy as jnp
from jax import lax
from jax.experimental import pallas as pl
from jax.experimental.pallas import tpu as pltpu
from jax.sharding import Mesh, PartitionSpec as P

KV_HEADS = 5
GROUP = 5
HEAD = 64
INNER = 3200
STATE = 16
CONV = 4
WINDOW = 1024
STEP = 64
CHAIN = 64
SPREAD = 32
LANES = 128
MIB = 1024 * 1024
LOG2 = 0.6931471805599453

epsilon = 1e-06


def row(ref, index, like):
    return jnp.broadcast_to(ref[pl.ds(index, 1), :], like.shape)


def column(block, index, like):
    return jnp.broadcast_to(block[:, index : index + 1], like.shape)


def turned(block, start):
    return pltpu.roll(block, lax.rem(LANES - start, LANES), 1)


def local_kernel(dt_ref, u_ref, b_ref, rate_ref, out_ref):
    @pl.when(pl.program_id(0) == 0)
    def _():
        out_ref[...] = jnp.zeros_like(out_ref)

    rates = rate_ref[...]
    b_all = b_ref[...]

    def block(j, state):
        start = pl.multiple_of(j * STEP, STEP)
        b_cols = turned(b_all, start)
        for i in range(STEP):
            decay = jnp.exp2(row(dt_ref, start + i, state) * rates)
            state = decay * state + row(u_ref, start + i, state) * column(b_cols, i, state)
        return state

    out_ref[...] = lax.fori_loop(0, dt_ref.shape[0] // STEP, block, out_ref[...])


def value_kernel(dt_ref, u_ref, b_ref, c_ref, rate_ref, enter_ref, out_ref, kept_ref, state_ref):
    @pl.when(pl.program_id(0) == 0)
    def _():
        state_ref[...] = enter_ref[...]

    rates = rate_ref[...]
    b_all = b_ref[...]
    c_all = c_ref[...]

    def block(j, state):
        start = pl.multiple_of(j * STEP, STEP)
        b_cols = turned(b_all, start)
        c_cols = turned(c_all, start)
        rows = []
        for i in range(STEP):
            kept_ref[start + i] = state
            decay = jnp.exp2(row(dt_ref, start + i, state) * rates)
            state = decay * state + row(u_ref, start + i, state) * column(b_cols, i, state)
            rows.append(jnp.sum(state * column(c_cols, i, state), 0, keepdims=True))
        out_ref[pl.ds(start, STEP), :] = jnp.concatenate(rows, 0)
        return state

    state_ref[...] = lax.fori_loop(0, dt_ref.shape[0] // STEP, block, state_ref[...])


def push_kernel(dt_ref, dy_ref, c_ref, rate_ref, out_ref):
    @pl.when(pl.program_id(0) == 0)
    def _():
        out_ref[...] = jnp.zeros_like(out_ref)

    rates = rate_ref[...]
    c_all = c_ref[...]
    count = dt_ref.shape[0] // STEP

    def block(k, push):
        start = pl.multiple_of((count - 1 - k) * STEP, STEP)
        c_cols = turned(c_all, start)
        for i in range(STEP - 1, -1, -1):
            decay = jnp.exp2(row(dt_ref, start + i, push) * rates)
            push = decay * (push + row(dy_ref, start + i, push) * column(c_cols, i, push))
        return push

    out_ref[...] = lax.fori_loop(0, count, block, out_ref[...])


def back_kernel(
    dt_ref,
    u_ref,
    dy_ref,
    b_ref,
    c_ref,
    rate_ref,
    kept_ref,
    future_ref,
    first_ref,
    second_ref,
    db_ref,
    dc_ref,
    drate_ref,
    push_ref,
    adjoint_ref,
    moved_ref,
    db_wide_ref,
    dc_wide_ref,
):
    @pl.when(pl.program_id(0) == 0)
    def _():
        push_ref[...] = future_ref[...]
        drate_ref[...] = jnp.zeros_like(drate_ref)

    rates = rate_ref[...]
    b_all = b_ref[...]
    c_all = c_ref[...]
    rows = dt_ref.shape[0]
    states = rates.shape[0]

    def chain(k, push):
        start = pl.multiple_of((rows // CHAIN - 1 - k) * CHAIN, CHAIN)
        c_cols = turned(c_all, start)
        for i in range(CHAIN - 1, -1, -1):
            decay = jnp.exp2(row(dt_ref, start + i, push) * rates)
            adjoint = push + row(dy_ref, start + i, push) * column(c_cols, i, push)
            adjoint_ref[start + i] = adjoint
            moved_ref[start + i] = decay * kept_ref[start + i]
            push = decay * adjoint
        return push

    push_ref[...] = lax.fori_loop(0, rows // CHAIN, chain, push_ref[...])

    def fold(wide):
        parts = wide[:, :LANES]
        for first in range(LANES, wide.shape[1], LANES):
            parts = parts + wide[:, first : first + LANES]
        return parts

    def spread(k, drate):
        start = pl.multiple_of(k * SPREAD, SPREAD)
        b_cols = turned(b_all, start)
        first_rows = []
        second_rows = []
        for i in range(SPREAD):
            adjoint = adjoint_ref[start + i]
            moved = moved_ref[start + i]
            u_wide = row(u_ref, start + i, moved)
            b_wide = column(b_cols, i, moved)
            dc_wide_ref[start + i] = fold(row(dy_ref, start + i, moved) * (moved + u_wide * b_wide))
            db_wide_ref[start + i] = fold(adjoint * u_wide)
            mixed = adjoint * moved
            drate = drate + row(dt_ref, start + i, moved) * mixed
            first_rows.append(jnp.sum(rates * mixed, 0, keepdims=True))
            second_rows.append(jnp.sum(adjoint * b_wide, 0, keepdims=True))
        first_ref[pl.ds(start, SPREAD), :] = jnp.concatenate(first_rows, 0)
        second_ref[pl.ds(start, SPREAD), :] = jnp.concatenate(second_rows, 0)
        return drate

    drate_ref[...] = lax.fori_loop(0, rows // SPREAD, spread, drate_ref[...])
    ones = jnp.ones((LANES, LANES), jnp.bfloat16)
    place = lax.broadcasted_iota(jnp.int32, (rows, states, LANES), 0)
    lane = lax.broadcasted_iota(jnp.int32, (rows, states, LANES), 2)
    for wide_ref, out_ref in ((db_wide_ref, db_ref), (dc_wide_ref, dc_ref)):
        wide = wide_ref[...].reshape(rows * states, LANES)
        top = wide.astype(jnp.bfloat16)
        rest = (wide - top.astype(jnp.float32)).astype(jnp.bfloat16)
        total = jnp.dot(top, ones, preferred_element_type=jnp.float32) + jnp.dot(
            rest, ones, preferred_element_type=jnp.float32
        )
        held = jnp.where(place == lane, total.reshape(rows, states, LANES), 0.0)
        out_ref[...] = jnp.sum(held, 0)


def whole(shape):
    return pl.BlockSpec(shape, lambda s: (0,) * len(shape))


def params():
    return pltpu.CompilerParams(
        dimension_semantics=("arbitrary",), vmem_limit_bytes=40 * MIB
    )


def cost(rows, width, states, ops):
    return pl.CostEstimate(
        flops=rows * width * states * ops,
        bytes_accessed=rows * width * 16,
        transcendentals=rows * width * states,
    )


def real(*shape):
    return jax.ShapeDtypeStruct(shape, jnp.float32)


def local_scan(dt, u, b_t, rates):
    rows, width = dt.shape
    states = rates.shape[0]
    by_row = pl.BlockSpec((LANES, width), lambda s: (s, 0))
    by_lane = pl.BlockSpec((states, LANES), lambda s: (0, s))
    return pl.pallas_call(
        local_kernel,
        grid=(rows // LANES,),
        in_specs=[by_row, by_row, by_lane, whole((states, width))],
        out_specs=whole((states, width)),
        out_shape=real(states, width),
        compiler_params=params(),
        cost_estimate=cost(rows, width, states, 6),
        name="scan_local",
    )(dt, u, b_t, rates)


def value_scan(dt, u, b_t, c_t, rates, entering):
    rows, width = dt.shape
    states = rates.shape[0]
    by_row = pl.BlockSpec((LANES, width), lambda s: (s, 0))
    by_lane = pl.BlockSpec((states, LANES), lambda s: (0, s))
    wide = whole((states, width))
    return pl.pallas_call(
        value_kernel,
        grid=(rows // LANES,),
        in_specs=[by_row, by_row, by_lane, by_lane, wide, wide],
        out_specs=[by_row, pl.BlockSpec((LANES, states, width), lambda s: (s, 0, 0))],
        out_shape=[real(rows, width), real(rows, states, width)],
        scratch_shapes=[pltpu.VMEM((states, width), jnp.float32)],
        compiler_params=params(),
        cost_estimate=cost(rows, width, states, 8),
        name="scan_value",
    )(dt, u, b_t, c_t, rates, entering)


def push_scan(dt, dy, c_t, rates):
    rows, width = dt.shape
    states = rates.shape[0]
    last = rows // LANES - 1
    by_row = pl.BlockSpec((LANES, width), lambda s: (last - s, 0))
    by_lane = pl.BlockSpec((states, LANES), lambda s: (0, last - s))
    wide = whole((states, width))
    return pl.pallas_call(
        push_kernel,
        grid=(rows // LANES,),
        in_specs=[by_row, by_row, by_lane, wide],
        out_specs=wide,
        out_shape=real(states, width),
        compiler_params=params(),
        cost_estimate=cost(rows, width, states, 6),
        name="scan_push",
    )(dt, dy, c_t, rates)


def back_scan(dt, u, dy, b_t, c_t, rates, kept, future):
    rows, width = dt.shape
    states = rates.shape[0]
    last = rows // LANES - 1
    by_row = pl.BlockSpec((LANES, width), lambda s: (last - s, 0))
    by_lane = pl.BlockSpec((states, LANES), lambda s: (0, last - s))
    held = pl.BlockSpec((LANES, states, width), lambda s: (last - s, 0, 0))
    wide = whole((states, width))
    return pl.pallas_call(
        back_kernel,
        grid=(rows // LANES,),
        in_specs=[by_row, by_row, by_row, by_lane, by_lane, wide, held, wide],
        out_specs=[by_row, by_row, by_lane, by_lane, wide],
        out_shape=[
            real(rows, width),
            real(rows, width),
            real(states, rows),
            real(states, rows),
            real(states, width),
        ],
        scratch_shapes=[
            pltpu.VMEM((states, width), jnp.float32),
            pltpu.VMEM((LANES, states, width), jnp.float32),
            pltpu.VMEM((LANES, states, width), jnp.float32),
            pltpu.VMEM((LANES, states, LANES), jnp.float32),
            pltpu.VMEM((LANES, states, LANES), jnp.float32),
        ],
        compiler_params=params(),
        cost_estimate=cost(rows, width, states, 20),
        name="scan_back",
    )(dt, u, dy, b_t, c_t, rates, kept, future)

def stacked_heads(ref, head, group):
    first = head * group * HEAD
    parts = [ref[:, first + g * HEAD : first + (g + 1) * HEAD] for g in range(group)]
    return jnp.concatenate(parts, 0)


def flat_heads(value, group):
    rows = value.shape[0] // group
    return jnp.concatenate([value[g * rows : (g + 1) * rows] for g in range(group)], 1)


def over(left, right):
    return lax.dot_general(
        left, right, (((1,), (1,)), ((), ())), preferred_element_type=jnp.float32
    )


def down(left, right):
    return lax.dot_general(
        left, right, (((0,), (0,)), ((), ())), preferred_element_type=jnp.float32
    )


def biased_scores(queries, keys, bias, scale):
    scores = over(queries, keys)
    tokens = bias.shape[0]
    return (scores.reshape(-1, tokens, scores.shape[1]) * scale + bias[None]).reshape(scores.shape)


def attend_kernel(
    scale, first_ref, q_ref, mine_ref, other_ref, own_ref, bias_ref, out_ref, log_ref, all_ref
):
    bias = bias_ref[...]
    halo, width = mine_ref.shape
    half = first_ref[1]
    all_ref[half, :halo] = mine_ref[...]
    all_ref[1 - half, :halo] = other_ref[...]
    all_ref[0, halo:] = own_ref[:, :width]
    all_ref[1, halo:] = own_ref[:, width:]
    seen = pl.ds(pl.multiple_of(first_ref[0], HEAD), bias.shape[1])
    key_ref, value_ref = all_ref.at[0, seen], all_ref.at[1, seen]
    outs = []
    for head in range(KV_HEADS):
        queries = stacked_heads(q_ref, head, GROUP)
        keys = key_ref[:, head * HEAD : (head + 1) * HEAD]
        values = value_ref[:, head * HEAD : (head + 1) * HEAD]
        scores = biased_scores(queries, keys, bias, scale)
        row_max = jnp.max(scores, 1, keepdims=True)
        lifted = jnp.exp(scores - row_max)
        row_total = jnp.sum(lifted, 1, keepdims=True)
        probability = (lifted * (1.0 / row_total)).astype(jnp.bfloat16)
        outs.append(
            flat_heads(jnp.dot(probability, values, preferred_element_type=jnp.float32), GROUP)
        )
        log_ref[head] = row_max + jnp.log(row_total)
    out_ref[...] = jnp.concatenate(outs, 1)


def attend_back_kernel(
    scale, first_ref, q_ref, all_ref, bias_ref, log_ref, grad_ref, dq_ref, kept_ref, sent_ref
):
    bias = bias_ref[...]
    seen = pl.ds(pl.multiple_of(first_ref[0], HEAD), bias.shape[1])
    key_ref, value_ref = all_ref.at[0, seen], all_ref.at[1, seen]
    dqs, dks, dvs = [], [], []
    for head in range(KV_HEADS):
        queries = stacked_heads(q_ref, head, GROUP)
        grad = stacked_heads(grad_ref, head, GROUP)
        keys = key_ref[:, head * HEAD : (head + 1) * HEAD]
        values = value_ref[:, head * HEAD : (head + 1) * HEAD]
        probability = jnp.exp(biased_scores(queries, keys, bias, scale) - log_ref[head])
        prob_grad = over(grad, values)
        delta = jnp.sum(probability * prob_grad, 1, keepdims=True)
        score_grad = (probability * (prob_grad - delta)).astype(jnp.bfloat16)
        dq = jnp.dot(score_grad, keys, preferred_element_type=jnp.float32) * scale
        dqs.append(flat_heads(dq, GROUP))
        dks.append(down(score_grad, queries) * scale)
        dvs.append(down(probability.astype(jnp.bfloat16), grad))
    dq_ref[...] = jnp.concatenate(dqs, 1).astype(dq_ref.dtype)
    kept_ref[...] = jnp.zeros_like(kept_ref)
    sent_ref[...] = jnp.zeros_like(sent_ref)
    key_grad = jnp.concatenate(dks, 1).astype(kept_ref.dtype)
    value_grad = jnp.concatenate(dvs, 1).astype(kept_ref.dtype)

    @pl.when(first_ref[1] == 0)
    def _():
        kept_ref[seen] = key_grad
        sent_ref[seen] = value_grad

    @pl.when(first_ref[1] != 0)
    def _():
        kept_ref[seen] = value_grad
        sent_ref[seen] = key_grad


def attend_cost(rows, keys, products):
    return pl.CostEstimate(
        flops=2 * rows * GROUP * KV_HEADS * keys * HEAD * products,
        bytes_accessed=keys * KV_HEADS * HEAD * 12,
        transcendentals=rows * GROUP * KV_HEADS * keys,
    )


def in_smem():
    return pl.BlockSpec(memory_space=pltpu.SMEM)


def in_vmem(count):
    return [pl.BlockSpec(memory_space=pltpu.VMEM)] * count


def attend(first, queries, mine, other, own, bias, scale):
    rows, width = queries.shape
    keys = mine.shape[0] + own.shape[0]
    return pl.pallas_call(
        functools.partial(attend_kernel, scale),
        in_specs=[in_smem()] + in_vmem(5),
        out_shape=[
            real(rows, width),
            real(KV_HEADS, GROUP * rows, 1),
            jax.ShapeDtypeStruct((2, keys, KV_HEADS * HEAD), jnp.bfloat16),
        ],
        compiler_params=pltpu.CompilerParams(vmem_limit_bytes=40 * MIB),
        cost_estimate=attend_cost(rows, keys, 8),
        name="attend",
    )(first, queries, mine, other, own, bias)


def attend_back(first, queries, pair, bias, log_total, grad, scale):
    rows, width = queries.shape
    return pl.pallas_call(
        functools.partial(attend_back_kernel, scale),
        in_specs=[in_smem()] + in_vmem(5),
        out_shape=[
            jax.ShapeDtypeStruct((rows, width), jnp.bfloat16),
            jax.ShapeDtypeStruct(pair.shape[1:], jnp.bfloat16),
            jax.ShapeDtypeStruct(pair.shape[1:], jnp.bfloat16),
        ],
        compiler_params=pltpu.CompilerParams(vmem_limit_bytes=40 * MIB),
        cost_estimate=attend_cost(rows, pair.shape[1], 20),
        name="attend_back",
    )(first, queries, pair, bias, log_total, grad)


def weights_kernel(plan, *refs):
    out_ref = refs[-1]
    place = 0
    for left, right, first, columns, scale in plan:
        product = down(refs[left][...], refs[right][:, first : first + columns])
        out_ref[:, place : place + columns] = (product * scale).astype(out_ref.dtype)
        place += columns


def weight_grads(groups):
    lefts = [left for left, _, _ in groups]
    rights, plan = [], []
    for k, (_, scale, parts) in enumerate(groups):
        for right, first, columns in parts:
            plan.append((k, len(groups) + len(rights), first, columns, scale))
            rights.append(right)
    tokens, rows = lefts[0].shape
    wide = sum(part[3] for part in plan)
    tile = 256
    by_column = pl.BlockSpec((tokens, tile), lambda s: (0, s))
    return pl.pallas_call(
        functools.partial(weights_kernel, tuple(plan)),
        grid=(rows // tile,),
        in_specs=[by_column] * len(lefts) + [whole(right.shape) for right in rights],
        out_specs=pl.BlockSpec((tile, wide), lambda s: (s, 0)),
        out_shape=jax.ShapeDtypeStruct((rows, wide), jnp.bfloat16),
        compiler_params=params(),
        cost_estimate=pl.CostEstimate(
            flops=2 * tokens * rows * wide,
            bytes_accessed=2 * (2 * tokens * rows + tokens * wide + rows * wide),
            transcendentals=0,
        ),
        name="weight_grads",
    )(*lefts, *rights)


BLOCK = 64
PAD_ROWS = 32


def bf(value):
    return value.astype(jnp.bfloat16)


def fl(value):
    return value.astype(jnp.float32)


def dot(left, right, contract):
    return lax.dot_general(
        left, right, (contract, ((), ())), preferred_element_type=jnp.float32
    )


def mm(left, right):
    return dot(left, right, ((1,), (0,)))


def mm_t(left, right):
    return dot(left, right, ((1,), (1,)))


def t_mm(left, right):
    return dot(left, right, ((0,), (0,)))


def swap(value):
    return lax.ppermute(value, "w", [(0, 1), (1, 0)])


def pull(value, axis, amount):
    count = lax.axis_size(axis)
    return lax.ppermute(value, axis, [((i + amount) % count, i) for i in range(count)])


def around(value, axis):
    return [value] + [pull(value, axis, k) for k in range(1, lax.axis_size(axis))]


def ordered(pieces, axis):
    count = len(pieces)
    ring = jnp.stack(pieces + pieces[:-1])
    start = lax.rem(count - lax.axis_index(axis), count)
    return lax.dynamic_slice_in_dim(ring, start, count, 0)


def pick(value, index, dim):
    return lax.dynamic_index_in_dim(value, index, dim, keepdims=False)


def sum_group(value):
    value = value + fl(swap(bf(value)))
    sent = bf(value)
    for k in range(1, 4):
        value = value + fl(pull(sent, "y", k))
    return value


def finish_scatter(parts):
    total = parts[0]
    count = len(parts)
    for k in range(1, count):
        route = [(i, (i + k) % count) for i in range(count)]
        total = total + fl(lax.ppermute(bf(parts[k]), "y", route))
    return total


def scatter_true(part):
    rows, width = part.shape
    mine, half = lax.axis_index("y"), lax.axis_index("w")
    split = part.reshape(4, 2, rows // 8, width)
    summed = pick(split, half, 1) + fl(swap(bf(pick(split, 1 - half, 1))))
    return finish_scatter([pick(summed, lax.rem(mine + k, 4), 0) for k in range(4)])


def arrange_kernel(place_ref, own_ref, other_ref, out_ref):
    half = place_ref[1]
    out_ref[0, half] = own_ref[0]
    out_ref[0, 1 - half] = other_ref[0]


def arrange(own, other):
    count, rows, width = own.shape
    place = jnp.stack((lax.axis_index("y"), lax.axis_index("w")))
    block = pl.BlockSpec(
        (1, rows, width), lambda s, place_ref: (lax.rem(s + count - place_ref[0], count), 0, 0)
    )
    return pl.pallas_call(
        arrange_kernel,
        grid_spec=pltpu.PrefetchScalarGridSpec(
            num_scalar_prefetch=1,
            grid=(count,),
            in_specs=[block, block],
            out_specs=pl.BlockSpec((1, 2, rows, width), lambda s, place_ref: (s, 0, 0, 0)),
        ),
        out_shape=jax.ShapeDtypeStruct((count, 2, rows, width), own.dtype),
        compiler_params=params(),
        cost_estimate=pl.CostEstimate(
            flops=0, bytes_accessed=8 * count * rows * width, transcendentals=0
        ),
        name="arrange",
    )(place, own, other).reshape(-1, width)


def gather_true(value):
    stacked = jnp.stack(around(value, "y"))
    return arrange(stacked, swap(stacked))


def by_half(own, other, dim):
    first = lax.axis_index("w") == 0
    return jnp.concatenate((jnp.where(first, own, other), jnp.where(first, other, own)), dim)


def exchange(pieces, axes):
    return lax.all_to_all(pieces, axes, 0, 0)


def exchange_near(blocks):
    mine = lax.axis_index("y")
    pieces = [pick(blocks, mine, 0)]
    for k in range(1, 4):
        sent = pick(blocks, lax.rem(mine + 4 - k, 4), 0)
        pieces.append(lax.ppermute(sent, "y", [(i, (i - k) % 4) for i in range(4)]))
    return ordered(pieces, "y")


def entering(state, steps, rates, backward):
    states = rates.shape[0]
    value = jnp.concatenate((state, steps), 0)
    count = lax.axis_size("x") * lax.axis_size("z")
    mine = lax.axis_index(("x", "z"))
    pieces = exchange(jnp.broadcast_to(value[None], (count,) + value.shape), ("x", "z"))
    before = jnp.zeros_like(state)
    for k in range(count - 1, 0, -1) if backward else range(count - 1):
        ahead = k > mine if backward else k < mine
        moved = jnp.exp(rates * pieces[k, states:]) * before + pieces[k, :states]
        before = jnp.where(ahead, moved, before)
    return before


def from_behind(block, axes, distance):
    count = 1
    for axis in axes:
        count *= lax.axis_size(axis)
    route = [(i - distance, i) for i in range(count) if 0 <= i - distance < count]
    return lax.ppermute(block, axes, route)


def from_earlier(block):
    groups = ("x", "z")
    mine = lax.axis_index("y")
    behind = from_behind(block, groups, 1)
    beyond = from_behind(block, groups, 2)
    near, far = [], []
    for k in range(1, 4):
        wraps = mine + k >= 4
        sent = jnp.concatenate(
            (jnp.where(wraps, beyond, behind), jnp.where(wraps, behind, block)), 0
        )
        got = lax.ppermute(sent, "y", [(i, (i + k) % 4) for i in range(4)])
        far.append(got[: block.shape[0]])
        near.append(got[block.shape[0] :])
    return jnp.concatenate([beyond] + far[::-1] + [behind] + near[::-1], 0)


def to_earlier(grads, rows):
    groups = ("x", "z")
    mine = lax.axis_index("y")
    block = [grads[k * rows : (k + 1) * rows] for k in range(9)]
    own, behind, beyond = block[8], block[4], block[0]
    for k in range(1, 4):
        sent = bf(jnp.concatenate((block[4 - k], block[8 - k]), 0))
        got = fl(lax.ppermute(sent, "y", [(i, (i - k) % 4) for i in range(4)]))
        far, near = got[:rows], got[rows:]
        wraps = mine + k >= 4
        own = own + jnp.where(wraps, 0.0, near)
        behind = behind + jnp.where(wraps, near, far)
        beyond = beyond + jnp.where(wraps, far, 0.0)
    return (
        own
        + fl(from_behind(bf(behind), groups, -1))
        + fl(from_behind(bf(beyond), groups, -2))
    )


def selector(width):
    place = jnp.arange(width, dtype=jnp.int32)
    block = width // BLOCK
    target = place + (PAD_ROWS - block) * (place // block)
    return bf(target[:, None] == jnp.arange(BLOCK * PAD_ROWS, dtype=jnp.int32)[None])


def pad_gain(gain):
    block = gain.shape[0] // BLOCK
    return jnp.pad(gain.reshape(BLOCK, block), ((0, 0), (0, PAD_ROWS - block))).reshape(-1)


def trim_gain(gain, width):
    return gain.reshape(BLOCK, PAD_ROWS)[:, : width // BLOCK].reshape(-1)


def trim_wide(value, chosen):
    top = lax.reduce_precision(value, 8, 7)
    return mm_t(bf(top), chosen) + mm_t(bf(value - top), chosen)


def norm_apply(values, gain):
    return values * lax.rsqrt(jnp.mean(values * values, -1, keepdims=True) + epsilon) * gain


def norm_scale(values, width):
    return lax.rsqrt(jnp.sum(values * values, -1, keepdims=True) / width + epsilon)


def norm_back(values, scale, gain, grad, width):
    pushed = grad * gain
    along = jnp.sum(pushed * values, -1, keepdims=True) / width
    return pushed * scale - values * (scale * scale * scale) * along, jnp.sum(
        grad * values * scale, 0
    )


def swiglu_gate(gate_part, up_part):
    return jax.nn.silu(gate_part) * up_part


def widen(value, dim, size):
    pads = [(0, 0)] * value.ndim
    pads[dim] = (0, size - value.shape[dim])
    return jnp.pad(value, pads)


def round_up(value, unit):
    return -(-value // unit) * unit


def chunked(weight):
    rows, parts, columns = weight.shape
    wide = round_up(columns // 4, 128)
    cut = widen(weight.reshape(rows, parts, 4, columns // 4), 3, wide)
    cut = jnp.transpose(cut, (2, 0, 1, 3)).reshape(4, rows, parts * wide)
    return widen(cut, 1, PAD_ROWS)


def unchunked(grad, rows, parts, columns):
    wide = grad.shape[2] // parts
    cut = grad[:, :rows].reshape(4, rows, parts, wide)[..., : columns // 4]
    return fl(jnp.transpose(cut, (1, 2, 0, 3)).reshape(rows, parts, columns))


def to_chunks(packed):
    moved = lax.all_to_all(packed, "y", 0, 0)
    return moved.reshape(-1, packed.shape[-1])


def gather_rows(rows):
    return lax.all_gather(rows, ("x", "z"), axis=0, tiled=True)


def settle(grad):
    rows = lax.psum_scatter(bf(grad), ("x", "z"), scatter_dimension=0, tiled=True)
    return rows.reshape(4, -1, rows.shape[-1])


def conv_apply(extended, conv_taps, conv_bias):
    tap_count = conv_taps.shape[0]
    out_rows = extended.shape[0] - tap_count + 1
    summed = conv_bias + conv_taps[0] * extended[0:out_rows]
    for offset in range(1, tap_count):
        summed = summed + conv_taps[offset] * extended[offset : offset + out_rows]
    return jax.nn.silu(summed)


def shards(
    tokens,
    norm_gain,
    qkv_weight,
    heads_gain,
    mamba_in,
    conv_weight,
    conv_bias,
    state_proj,
    step_proj,
    step_bias,
    decay_log,
    skip_gain,
    mamba_gain,
    heads_out,
    mamba_out,
    mlp_gain,
    gate_up,
    down_proj,
    cotangent,
):
    tok_rows, width = tokens.shape
    shard_rows = qkv_weight.shape[0]
    inner_half = conv_weight.shape[1]
    inner = inner_half // 4
    lanes = round_up(inner, 128)
    hidden_half = gate_up.shape[2]
    hidden = round_up(hidden_half // 4, 128)
    heads_width = KV_HEADS * GROUP * HEAD
    kv_width = KV_HEADS * HEAD
    half_width = heads_width // 2
    qkv_half = qkv_weight.shape[1] // 2
    halo_count = WINDOW // tok_rows
    score_scale = HEAD ** (-0.5)
    x_pos, z_pos = lax.axis_index("x"), lax.axis_index("z")
    y_pos, w_pos = lax.axis_index("y"), lax.axis_index("w")
    group_axes, all_axes = ("x", "z"), ("x", "z", "y")
    own_rows = tok_rows // 2
    rank = step_proj.shape[0]

    def own_half(value, dim=0):
        size = value.shape[dim] // 2
        return lax.dynamic_slice_in_dim(value, w_pos * size, size, dim)

    def other_half(value, dim=0):
        size = value.shape[dim] // 2
        return lax.dynamic_slice_in_dim(value, (1 - w_pos) * size, size, dim)

    def own_block(value):
        return lax.dynamic_slice_in_dim(value, y_pos * tok_rows, tok_rows, 0)

    def channels(value, dim):
        part = lax.dynamic_slice_in_dim(value, y_pos * inner, inner, dim)
        return widen(fl(part), dim, lanes)

    qkv_wide, hout_wide = round_up(qkv_half // 4, 128), round_up(half_width // 4, 128)
    in_wide = 2 * lanes + qkv_wide
    early_full = gather_rows(
        to_chunks(
            jnp.concatenate(
                (
                    chunked(mamba_in),
                    chunked(own_half(qkv_weight, 1)[:, None]),
                    chunked(mamba_out[:, None]),
                ),
                2,
            )
        )
    )
    hout_full = lax.all_gather(widen(heads_out, 0, PAD_ROWS), all_axes, axis=0, tiled=True)
    late_full = gather_rows(
        to_chunks(jnp.concatenate((chunked(gate_up), chunked(down_proj[:, None])), 2))
    )
    gu_full = late_full[:, : 2 * hidden]
    down_full = late_full[:, 2 * hidden :]

    def to_tokens(chunk, columns):
        moved = lax.all_to_all(chunk.reshape(4, tok_rows, -1), "y", 0, 0)
        return jnp.transpose(moved[:, :, : columns // 4], (1, 0, 2)).reshape(tok_rows, columns)

    def to_columns(parts):
        cuts = [widen(rows.reshape(tok_rows, 4, -1), 2, wide) for rows, wide in parts]
        return to_chunks(jnp.transpose(jnp.concatenate(cuts, 2), (1, 0, 2)))

    chosen = selector(width)
    gain_first = pad_gain(norm_gain)
    gain_mid = pad_gain(mlp_gain)
    tokens_group = ordered(around(tokens, "y"), "y").reshape(4 * tok_rows, width)
    residual = mm(tokens_group, chosen)
    scale_first = norm_scale(residual, width)
    normed = bf(residual * scale_first * gain_first)

    cot_own = bf(mm(own_half(cotangent), chosen))
    early_full, cot_all = lax.optimization_barrier((early_full, gather_true(cot_own)))
    in_full = early_full[:, :in_wide]
    mout_full = early_full[:, in_wide:]

    mixed_in = bf(mm(normed, in_full))
    conv_in = mixed_in[:, :lanes]
    gate_float = fl(mixed_in[:, lanes : 2 * lanes])
    tail = from_behind(conv_in[-(CONV - 1) :], group_axes, 1)
    extended = fl(jnp.concatenate((tail, conv_in), 0))
    conv_taps = channels(conv_weight, 1)
    conv_shift = channels(conv_bias, 0)
    acted_b = bf(conv_apply(extended, conv_taps, conv_shift))
    acted = fl(acted_b)
    state_weight = bf(channels(state_proj, 0))
    state_t = sum_group(dot(state_weight, acted_b, ((0,), (1,))))
    low_rank_t = bf(state_t[:rank])
    input_t = state_t[rank : rank + STATE]
    output_t = state_t[rank + STATE :]
    step_weight = bf(channels(step_proj, 1))
    step_pre = t_mm(low_rank_t, step_weight) + channels(step_bias, 0)
    steps = jax.nn.softplus(step_pre)
    rates = -jnp.exp(channels(decay_log, 0)).T
    fast_rates = rates * (1.0 / LOG2)
    drive = steps * acted
    step_total = jnp.sum(steps, 0, keepdims=True)
    local_state = local_scan(steps, drive, input_t, fast_rates)
    carry_in = entering(local_state, step_total, rates, False)

    first_pos = (lax.axis_index(all_axes)) * tok_rows
    projected_half = to_tokens(mixed_in[:, 2 * lanes :], qkv_half)
    projected = by_half(projected_half, swap(projected_half), 1)
    own_first = w_pos * own_rows
    queries = own_half(projected[:, :heads_width])
    own_pair = projected[:, heads_width:]
    sent = own_half(own_pair, 1)
    halo_half = from_earlier(sent)
    seen = WINDOW + own_rows
    key_place = jnp.arange(seen, dtype=jnp.int32)[None]
    query_place = jnp.arange(own_rows, dtype=jnp.int32)[:, None]
    visible = (
        (key_place > query_place)
        & (key_place <= query_place + WINDOW)
        & (key_place >= WINDOW - first_pos - own_first)
    )
    bias = jnp.where(visible, 0.0, -1e30).astype(jnp.float32)
    place = jnp.stack((own_first, w_pos))
    heads_value, log_total, pair_all = attend(
        place, queries, halo_half, swap(halo_half), own_pair, bias, score_scale
    )
    heads_normed = bf(norm_apply(heads_value, heads_gain))
    heads_half = by_half(own_half(heads_normed, 1), swap(other_half(heads_normed, 1)), 0)
    heads_part = mm_t(heads_half, hout_full)
    heads_mixed = own_half(heads_part) + fl(swap(bf(other_half(heads_part))))

    skip = channels(skip_gain, 0)
    scanned, kept = value_scan(steps, drive, input_t, output_t, fast_rates, carry_in)
    ssm_value = scanned + skip * acted
    gate_act = jax.nn.silu(gate_float)
    gated = ssm_value * gate_act
    gain_mamba = channels(mamba_gain, 0)
    lane = lax.broadcasted_iota(jnp.int32, (1, BLOCK * PAD_ROWS), 1)

    def tuck(value, extras):
        for k, extra in enumerate(extras):
            value = jnp.where(lane == shard_rows + k, extra, value)
        return value

    squares = jnp.sum(gated * gated, -1, keepdims=True)
    unscaled = scatter_true(tuck(mm_t(bf(gated * gain_mamba), mout_full), (squares,)))
    mamba_scale_own = lax.rsqrt(unscaled[:, shard_rows : shard_rows + 1] / INNER + epsilon)
    unscaled = jnp.where(lane == shard_rows, 0.0, unscaled)
    mixer = 0.5 * (unscaled * mamba_scale_own + heads_mixed)
    own_tokens = mm(own_half(tokens), chosen)
    middle = own_tokens + mixer
    scale_mid = norm_scale(middle, width)

    normed_mid = gather_true(bf(middle * scale_mid * gain_mid))
    gate_values = mm(normed_mid, gu_full)
    gate_part, up_part = gate_values[:, :hidden], gate_values[:, hidden:]
    hidden_b = bf(swiglu_gate(gate_part, up_part))
    mlp_part = mm_t(hidden_b, down_full)
    hidden_grad = mm(cot_all, down_full)
    gate_grad, up_grad = jax.vjp(swiglu_gate, gate_part, up_part)[1](hidden_grad)
    gate_values_grad = bf(jnp.concatenate((gate_grad, up_grad), 1))
    ffn_grad = weight_grads(
        (
            (normed_mid, 1.0, ((gate_values_grad, 0, 2 * hidden),)),
            (cot_all, 1.0, ((hidden_b, 0, hidden),)),
        )
    )
    mid_grad = scatter_true(mm_t(gate_values_grad, gu_full))
    mid_grad, ffn_grad = lax.optimization_barrier((mid_grad, ffn_grad))
    ffn_rows = settle(ffn_grad)
    mid_back, mlp_gain_grad = norm_back(middle, scale_mid, gain_mid, mid_grad, width)
    middle_grad = fl(cot_own) + mid_back

    mixer_grad_own = bf(middle_grad)
    row_total_own = 0.5 * jnp.sum(fl(mixer_grad_own) * unscaled, -1, keepdims=True)
    extras = []
    for value in (mamba_scale_own, row_total_own):
        top = lax.reduce_precision(value, 8, 7)
        extras += [bf(top), bf(value - top)]
    mixer_grad = gather_true(tuck(mixer_grad_own, extras))
    tucked = fl(mixer_grad[:, shard_rows : shard_rows + 4])
    mamba_scale = tucked[:, 0:1] + tucked[:, 1:2]
    row_total = tucked[:, 2:3] + tucked[:, 3:4]
    mamba_normed = bf(gated * mamba_scale * gain_mamba)
    mamba_normed_grad = 0.5 * mm(mixer_grad, mout_full)
    half_grad = bf(0.5 * mm(own_block(mixer_grad), hout_full))
    gated_grad = (
        mamba_normed_grad * gain_mamba * mamba_scale
        - gated * mamba_scale**3 * row_total / INNER
    )
    mamba_gain_grad = jnp.sum(mamba_normed_grad * gated * mamba_scale, 0)
    ssm_grad = gated_grad * gate_act
    gate_in_grad = jax.vjp(jax.nn.silu, gate_float)[1](gated_grad * ssm_value)[0]
    gate_in_grad = bf(gate_in_grad)
    push = push_scan(steps, ssm_grad, output_t, fast_rates)
    push, half_grad = lax.optimization_barrier((push, half_grad))
    future = entering(push, step_total, rates, True)

    heads_normed_grad = by_half(own_half(half_grad), swap(other_half(half_grad)), 1)
    heads_value_grad, heads_gain_grad = jax.vjp(norm_apply, heads_value, heads_gain)[1](
        fl(heads_normed_grad)
    )
    query_grad, kept_grad, sent_grad = attend_back(
        place, queries, pair_all, bias, log_total, bf(heads_value_grad), score_scale
    )
    pair_half = fl(kept_grad) + fl(swap(sent_grad))
    own_pair_grad = to_earlier(pair_half, tok_rows)
    own_pair_grad = bf(own_pair_grad)
    projected_grad = jnp.concatenate(
        (
            by_half(query_grad, swap(query_grad), 0),
            by_half(own_pair_grad, swap(own_pair_grad), 1),
        ),
        1,
    )
    projected_grad_half = own_half(projected_grad, 1)
    both_chunks = to_columns(((heads_half, hout_wide), (projected_grad_half, qkv_wide)))
    out_grad = weight_grads(
        (
            (mixer_grad, 0.5, ((mamba_normed, 0, lanes), (both_chunks, 0, hout_wide))),
            (normed, 1.0, ((gate_in_grad, 0, lanes), (both_chunks, hout_wide, qkv_wide))),
        )
    )
    mlp = lax.psum_scatter(bf(mlp_part), ("y", "w"), scatter_dimension=0, tiled=True)

    first_part, second_part, input_grad_t, output_grad_t, rate_grad = back_scan(
        steps, drive, ssm_grad, input_t, output_t, fast_rates, kept, future
    )
    step_grad = LOG2 * first_part + acted * second_part
    acted_core_grad = steps * second_part + skip * ssm_grad
    skip_grad = jnp.sum(ssm_grad * acted, 0)
    step_pre_grad = step_grad * jax.nn.sigmoid(step_pre)
    step_bias_grad = jnp.sum(step_pre_grad, 0)
    step_pre_b = bf(step_pre_grad)
    step_proj_grad = mm(low_rank_t, step_pre_b)
    low_rank_grad_t = mm_t(step_weight, step_pre_b)
    state_grad_t = sum_group(jnp.concatenate((low_rank_grad_t, input_grad_t, output_grad_t), 0))
    state_grad_t, out_grad, ffn_rows, mlp = lax.optimization_barrier(
        (bf(state_grad_t), out_grad, ffn_rows, mlp)
    )
    out_rows = settle(out_grad)
    state_proj_grad_t = mm(state_grad_t, acted_b)
    acted_grad = acted_core_grad + dot(state_grad_t, state_weight, ((0,), (1,)))
    extended_grad, conv_weight_grad, conv_bias_grad = jax.vjp(
        conv_apply, extended, conv_taps, conv_shift
    )[1](acted_grad)
    returned = from_behind(extended_grad[: CONV - 1], group_axes, -1)
    group_rows = 4 * tok_rows
    conv_in_grad = jnp.concatenate(
        (extended_grad[CONV - 1 : group_rows], extended_grad[group_rows:] + returned), 0
    )
    conv_in_grad = bf(conv_in_grad)
    out_half = bf(mm_t(bf(middle + fl(mlp)), chosen))
    layer_out = by_half(out_half, swap(out_half), 0)
    wide_gain = BLOCK * PAD_ROWS
    early_gains = jnp.concatenate((mlp_gain_grad, widen(heads_gain_grad, 0, wide_gain)))
    early_gains = early_gains.reshape(-1, lanes)
    early_gains = early_gains + swap(early_gains)
    groups = lax.axis_size("x") * lax.axis_size("z")
    inner_rows = jnp.concatenate(
        (
            rate_grad * rates,
            state_proj_grad_t,
            conv_weight_grad,
            step_proj_grad,
            conv_bias_grad[None],
            step_bias_grad[None],
            skip_grad[None],
            mamba_gain_grad[None],
        ),
        0,
    )
    share = -(-inner_rows.shape[0] // groups)
    small = jnp.concatenate(
        (
            bf(widen(inner_rows, 0, share * groups)).reshape(groups, share, lanes),
            bf(widen(early_gains, 0, groups))[:, None],
        ),
        1,
    )
    conv_grad = bf(t_mm(normed, conv_in_grad)).reshape(groups, -1, lanes)
    share = small.shape[1]
    sent, conv_in_grad = lax.optimization_barrier(
        (jnp.concatenate((conv_grad, small), 1), conv_in_grad)
    )
    both = bf(jnp.sum(fl(exchange(sent, group_axes)), 0))
    conv_rows, small = both[:-share], both[-share:]
    back_grad = jnp.concatenate((conv_in_grad, gate_in_grad, both_chunks[:, hout_wide:]), 1)
    normed_grad = scatter_true(mm_t(back_grad, in_full))
    own_scale = own_half(own_block(scale_first))
    first_back, norm_gain_grad = norm_back(
        own_tokens, own_scale, gain_first, normed_grad, width
    )
    tokens_half = trim_wide(middle_grad + first_back, chosen)
    tokens_grad = by_half(tokens_half, swap(tokens_half), 0)

    def to_all(rows):
        every = (groups * lax.axis_size("y"),)
        return exchange(jnp.broadcast_to(rows[None], every + rows.shape), all_axes)

    late_gain = norm_gain_grad.reshape(-1, lanes)
    late_gain = bf(late_gain + swap(late_gain))
    shared = to_all(jnp.concatenate((small, late_gain), 0))
    conv_moved = exchange_near(conv_rows.reshape(4, -1, lanes))
    out_moved = exchange_near(jnp.concatenate((ffn_rows, out_rows), 2))
    late_gain = jnp.sum(fl(shared[:, share:]), 0).reshape(-1)
    small = shared[:, :share].reshape(groups, -1, share, lanes)
    gains = jnp.sum(fl(small[: early_gains.shape[0], :, -1]), 1).reshape(2, -1)


    def taken(moved, first, wide, parts, columns):
        return unchunked(moved[:, :, first : first + wide], shard_rows, parts, columns)

    gu_settled = taken(out_moved, 0, 2 * hidden, 2, hidden_half)
    down_settled = taken(out_moved, 2 * hidden, hidden, 1, hidden_half)[:, 0]
    first = 3 * hidden
    mout_settled = taken(out_moved, first, lanes, 1, inner_half)[:, 0]
    hout_settled = taken(out_moved, first + lanes, hout_wide, 1, half_width)[:, 0]
    first = first + lanes + hout_wide
    gate_settled = taken(out_moved, first, lanes, 1, inner_half)
    conv_settled = taken(conv_moved, 0, lanes, 1, inner_half)
    in_settled = jnp.concatenate((conv_settled, gate_settled), 1)
    qkv_own = taken(out_moved, first + lanes, qkv_wide, 1, qkv_half)[:, 0]
    qkv_settled = by_half(qkv_own, swap(qkv_own), 1)

    by_channel = jnp.transpose(small[:, :, :-1, :inner], (0, 2, 1, 3)).reshape(-1, inner_half)
    by_channel = fl(by_channel)
    states_end = STATE + state_proj.shape[1]
    taps_end = states_end + CONV
    last = taps_end + rank
    return (
        layer_out,
        tokens_grad,
        trim_gain(late_gain, width),
        qkv_settled,
        gains[1, :heads_width],
        in_settled,
        by_channel[states_end:taps_end],
        by_channel[last],
        by_channel[STATE:states_end].T,
        by_channel[taps_end:last],
        by_channel[last + 1],
        by_channel[:STATE].T,
        by_channel[last + 2],
        by_channel[last + 3],
        hout_settled,
        mout_settled,
        trim_gain(gains[0], width),
        gu_settled,
        down_settled,
    )


def solution(mesh):
    split = Mesh(mesh.devices.reshape(4, 4, 4, 2), ("x", "z", "y", "w"))
    ctx = ("x", "z", "y")
    placed = (
        P(ctx, None),
        P(),
        P(ctx, None),
        P(),
        P(ctx, None, "w"),
        P(None, "w"),
        P("w"),
        P("w", None),
        P(None, "w"),
        P("w"),
        P("w", None),
        P("w"),
        P("w"),
        P(ctx, "w"),
        P(ctx, "w"),
        P(),
        P(ctx, None, "w"),
        P(ctx, "w"),
        P(ctx, None),
    )
    return jax.shard_map(
        shards,
        mesh=split,
        in_specs=placed,
        out_specs=(
            P(ctx, None),
            P(ctx, None),
            P(),
            P(ctx, None),
            P(),
            P(ctx, None, "w"),
            P(None, "w"),
            P("w"),
            P("w", None),
            P(None, "w"),
            P("w"),
            P("w", None),
            P("w"),
            P("w"),
            P(ctx, "w"),
            P(ctx, "w"),
            P(),
            P(ctx, None, "w"),
            P(ctx, "w"),
        ),
        check_vma=False,
    )
```
